32 devices in a mesh: dp: 8 (over y, x, core), mp: 4 (over z).
Axes of the slice: x: 2, y: 2, z: 4, core: 2. Of those that a mesh axis runs over, the one named last changes fastest.
Arguments:
- image_feats: bfloat16 [4096, 1152], P(('dp', 'mp')), may hold values from -6 to 6
- text_feats: bfloat16 [4096, 1152], P(('dp', 'mp')), may hold values from -6 to 6
- image_proj: bfloat16 [1152, 1152], replicated, may hold values from -0.1875 to 0.1875
- text_proj: bfloat16 [1152, 1152], replicated, may hold values from -0.1875 to 0.1875
- log_scale: float32 [1], replicated, may hold values from 3.6 to 4.3
- logit_bias: float32 [1], replicated, may hold values from -12 to -9
Outputs:
- loss: float32 [1], replicated
- image_proj_grad: float32 [1152, 1152], P(('dp', 'mp'))
- text_proj_grad: float32 [1152, 1152], P(('dp', 'mp'))
- log_scale_grad: float32 [1], replicated
- bias_grad: float32 [1], replicated
The draws below stay inside these ranges and needn't reach their ends.
All inputs are finite; a program needn't handle non-finite values.
Results may differ from the reference program's by a relative error of at most 0.0035.
Values may be sent and summed in bfloat16 or wider, within the bound.
No kernel may reach another device: no remote copies, remote signals or barrier semaphores. Data moves between devices by JAX's collectives and lax.ppermute only.
A program may use at most 128 MiB of HBM per device.

```python
import math
import jax
import jax.numpy as jnp
from jax import lax

WIDTH = 1152
BATCH = 4096


def steps_of(stream_key, dims, cuts, low, top_value):
    level = 1.0
    for dim, blocks in cuts:
        heights = jax.random.uniform(jax.random.fold_in(jax.random.fold_in(stream_key, 6), dim), (blocks,), jnp.float32, low / len(cuts), top_value / len(cuts))
        level = level * jnp.repeat(jnp.exp(heights), dims[dim] // blocks).reshape((-1,) + (1,) * (len(dims) - 1 - dim))
    return level


def normal_values(stream_key, shape, deviation, limit, shards=(), kind=jnp.bfloat16):
    loudness = steps_of(stream_key, shape, shards, -0.22, 0.18) if shards else 1.0
    drawn = jax.random.normal(stream_key, shape, jnp.float32) * deviation * loudness
    return jnp.minimum(jnp.maximum(drawn, -limit), limit).astype(kind)


def setup_inputs(seed: int = 0) -> dict:
    streams_of = jax.random.split(jax.random.key(seed), 7)
    return {
        "image_feats": normal_values(streams_of[0], (BATCH, WIDTH), 1.0, 6.0, ((0, 32),)),
        "text_feats": normal_values(streams_of[1], (BATCH, WIDTH), 1.0, 6.0, ((0, 32),)),
        "image_proj": normal_values(streams_of[2], (WIDTH, WIDTH), WIDTH ** -0.5, 0.1875),
        "text_proj": normal_values(streams_of[3], (WIDTH, WIDTH), WIDTH ** -0.5, 0.1875),
        "log_scale": jnp.clip(jax.random.uniform(streams_of[4], (1,), jnp.float32, 3.6, 4.3), 3.6, 4.3),
        "logit_bias": jnp.clip(jax.random.uniform(streams_of[5], (1,), jnp.float32, -12.0, -9.0), -12.0, -9.0),
    }


def normalize(features, projection):
    projected = jnp.dot(features, projection, preferred_element_type=jnp.float32)
    row_norm = jnp.sqrt(lax.optimization_barrier(jnp.sum(projected * projected, axis=-1, keepdims=True)) + 1e-06)
    return (projected / row_norm, row_norm)

def unnormalize(unit_rows, row_norm, unit_grad):
    inner_product = lax.optimization_barrier(jnp.sum(unit_rows * unit_grad, axis=-1, keepdims=True))
    return ((unit_grad - unit_rows * inner_product) / row_norm).astype(jnp.bfloat16)

def pair_terms(cosine, label_signs, logit_scale, bias_value):
    logits = logit_scale * cosine + bias_value
    losses = -jax.nn.log_sigmoid(label_signs * logits)
    pair_grads = -label_signs * jax.nn.sigmoid(-label_signs * logits)
    return (jnp.sum(losses), jnp.sum(pair_grads * logit_scale * cosine), jnp.sum(pair_grads), pair_grads.astype(jnp.bfloat16))

def reference(image_feats, text_feats, image_proj, text_proj, log_scale, logit_bias):
    image_unit, image_norm = normalize(image_feats, image_proj)
    text_unit, text_norm = normalize(text_feats, text_proj)
    image_half = image_unit.astype(jnp.bfloat16)
    text_half = text_unit.astype(jnp.bfloat16)
    logit_scale = jnp.exp(log_scale[0])
    bias_value = logit_bias[0]
    block_rows = math.gcd(BATCH, 512)
    columns = jnp.arange(BATCH, dtype=jnp.int32)

    def score_block(running, offset):
        text_grad, loss_sum, scale_sum, bias_sum = running
        row_block = lax.dynamic_slice_in_dim(image_half, offset, block_rows, 0)
        cosine = jnp.dot(row_block, text_half.T, preferred_element_type=jnp.float32)
        row_ids = offset + jnp.arange(block_rows, dtype=jnp.int32)
        label_signs = jnp.where(row_ids[:, None] == columns[None, :], 1.0, -1.0).astype(jnp.float32)
        loss_part, scale_part, bias_part, half_grads = pair_terms(cosine, label_signs, logit_scale, bias_value)
        image_grad = logit_scale * jnp.dot(half_grads, text_half, preferred_element_type=jnp.float32)
        text_grad = text_grad + logit_scale * jnp.dot(half_grads.T, row_block, preferred_element_type=jnp.float32)
        return ((text_grad, loss_sum + loss_part, scale_sum + scale_part, bias_sum + bias_part), image_grad)
    offsets = jnp.arange(BATCH // block_rows, dtype=jnp.int32) * block_rows
    starting = (jnp.zeros((BATCH, WIDTH), jnp.float32), jnp.zeros((), jnp.float32), jnp.zeros((), jnp.float32), jnp.zeros((), jnp.float32))
    finished, image_blocks = lax.scan(score_block, starting, offsets)
    text_grad, loss_sum, scale_sum, bias_sum = finished
    image_grad = image_blocks.reshape(BATCH, WIDTH)
    image_dy = unnormalize(image_unit, image_norm, image_grad)
    text_dy = unnormalize(text_unit, text_norm, text_grad)
    image_proj_grad = jnp.dot(image_feats.T, image_dy, preferred_element_type=jnp.float32)
    text_proj_grad = jnp.dot(text_feats.T, text_dy, preferred_element_type=jnp.float32)
    return ((loss_sum / BATCH).reshape(1), image_proj_grad, text_proj_grad, (scale_sum / BATCH).reshape(1), (bias_sum / BATCH).reshape(1))
```

```python
import functools
import math

import jax
import jax.numpy as jnp
from jax import lax
from jax.experimental import pallas as pl
from jax.experimental.pallas import tpu as pltpu
from jax.sharding import PartitionSpec as P

F32 = jnp.float32
BF16 = jnp.bfloat16
AXES = ("dp", "mp")


class Layout:
    def __init__(self, dp_size, mp_size):
        self.dp, self.mp = dp_size, mp_size
        self.units = dp_size * mp_size // 2
        self.side = math.isqrt(self.units)
        if self.side * self.side != self.units or self.side % mp_size:
            raise ValueError("unsupported mesh")

    def device(self, unit, core):
        return (2 * (unit // self.mp) + core) * self.mp + unit % self.mp

    def permutation(self, row_step, column_step, flip):
        s = self.side
        pairs = []
        for unit in range(self.units):
            row, column = divmod(unit, s)
            target = (row + row_step) % s * s + (column + column_step) % s
            for core in range(2):
                pairs.append((self.device(unit, core), self.device(target, core ^ flip)))
        return pairs


def block_kernel(
    side, shard_rows, tile, scalars, image_proj, text_proj, *refs
):
    shards = 2 * side
    image_shards, text_shards = refs[:shards], refs[shards : 2 * shards]
    outs = refs[2 * shards : 3 * shards - side]
    stats, feats, projs, other_half, dy, grad, sems = refs[3 * shards - side :]
    rows, width = dy.shape
    chunk = width // side
    mp_size = lax.axis_size("mp")
    dp_index, mp_index = lax.axis_index("dp"), lax.axis_index("mp")
    core = lax.rem(dp_index, 2)
    unit_row = (dp_index // 2 * mp_size + mp_index) // side
    scale, bias = scalars[0], scalars[1]

    copies = {}

    def start(name, source, target):
        copies[name] = pltpu.make_async_copy(source, target, sems.at[len(copies)])
        copies[name].start()

    start("text_proj", text_proj, projs.at[1 - core])
    start("image_proj", image_proj, projs.at[core])
    for i in range(shards):
        place = pl.ds(i * shard_rows, shard_rows)
        start(("text", i), text_shards[i], feats.at[1 - core, place])
        start(("image", i), image_shards[i], feats.at[core, place])
    for copy in copies.values():
        copy.wait()

    def project(which, place):
        raw = jnp.dot(feats[which, place, :], projs[which], preferred_element_type=F32)
        inverse = lax.rsqrt(jnp.sum(raw * raw, axis=-1, keepdims=True) + 1e-06)
        return raw * inverse, inverse

    @pl.loop(0, rows // tile)
    def _(i):
        place = pl.ds(pl.multiple_of(i * tile, tile), tile)
        unit, _ = project(1, place)
        other_half[place, :] = unit.astype(BF16)

    stats[...] = jnp.zeros_like(stats)

    def lanes(values):
        total = jnp.sum(values, axis=0, keepdims=True)
        return sum(total[:, j : j + 128] for j in range(0, total.shape[1], 128))

    @pl.loop(0, rows // tile)
    def _(i):
        place = pl.ds(pl.multiple_of(i * tile, tile), tile)
        unit, inverse = project(0, place)
        cosine = lax.dot_general(
            unit.astype(BF16), other_half[...], (((1,), (1,)), ((), ())), preferred_element_type=F32
        )
        logits = scale * cosine + bias
        small = jnp.exp(-jnp.abs(logits))
        inverse_sum = 1.0 / (1.0 + small)
        large_side = logits >= 0.0
        upper = jnp.where(large_side, inverse_sum, small * inverse_sum)
        lower = jnp.where(large_side, small * inverse_sum, inverse_sum)
        row_ids = i * tile + lax.broadcasted_iota(jnp.int32, (tile, 1), 0)
        row_ids = jnp.where(row_ids < 2 * shard_rows, row_ids, -1)
        equal = row_ids == lax.broadcasted_iota(jnp.int32, cosine.shape, 1)
        losses = jnp.maximum(jnp.where(equal, -logits, logits), 0.0) + jnp.log1p(small)
        pair_grads = jnp.where(equal, -lower, upper)
        half_grads = pair_grads.astype(BF16)
        stats[0:1, :] += lanes(losses)
        stats[1:2, :] += lanes(pair_grads * cosine)
        stats[2:3, :] += lanes(pair_grads)
        inner = jnp.sum(half_grads.astype(F32) * cosine, axis=-1, keepdims=True)
        grads = jnp.dot(half_grads, other_half[...], preferred_element_type=F32)
        dy[place, :] = ((grads - unit * inner) * (scale * inverse)).astype(BF16)

    stats[1:2, :] = stats[1:2, :] * scale
    for j in range(0, width, 128):
        grad[j : j + 128, :] = lax.dot_general(
            feats[0, :, j : j + 128], dy[...], (((0,), (0,)), ((), ())), preferred_element_type=F32
        )
    for t in range(side):
        first = pl.multiple_of(lax.rem(unit_row + t, side) * chunk, chunk)
        outs[t][...] = grad[pl.ds(first, chunk), :].astype(outs[t].dtype)


def block_grads(layout, scalars, image_proj, text_proj, image_shards, text_shards):
    side = layout.side
    shard_rows, width = image_shards[0].shape
    rows = 2 * side * shard_rows
    chunk = width // side
    tile = 256
    anywhere = pl.BlockSpec(memory_space=pl.ANY)
    vmem = pl.BlockSpec(memory_space=pltpu.VMEM)
    copies = 4 * side + 2
    return pl.pallas_call(
        functools.partial(block_kernel, side, shard_rows, tile),
        out_shape=[jax.ShapeDtypeStruct((chunk, width), F32)]
        + [jax.ShapeDtypeStruct((chunk, width), BF16)] * (side - 1)
        + [jax.ShapeDtypeStruct((8, 128), F32)],
        in_specs=[pl.BlockSpec(memory_space=pltpu.SMEM)] + [anywhere] * copies,
        out_specs=[vmem] * (side + 1),
        scratch_shapes=[
            pltpu.VMEM((2, rows, width), BF16),
            pltpu.VMEM((2, width, width), BF16),
            pltpu.VMEM((rows, width), BF16),
            pltpu.VMEM((rows, width), BF16),
            pltpu.VMEM((width, width), F32),
            pltpu.SemaphoreType.DMA((copies,)),
        ],
        compiler_params=pltpu.CompilerParams(vmem_limit_bytes=56 * 1024 * 1024),
        cost_estimate=pl.CostEstimate(
            flops=2 * rows * width * (2 * width + 2 * rows + width),
            bytes_accessed=4 * rows * width + 8 * width * width,
            transcendentals=3 * rows * rows,
        ),
        name="block",
    )(scalars, image_proj, text_proj, *image_shards, *text_shards)


def per_device(layout, image_feats, text_feats, image_proj, text_proj, log_scale, logit_bias):
    side, mp_size = layout.side, layout.mp
    own_rows, width = image_feats.shape
    devices = layout.dp * layout.mp
    out_rows = width // devices
    batch_total = own_rows * devices
    dp_index, mp_index = lax.axis_index("dp"), lax.axis_index("mp")
    core = dp_index % 2
    unit_column = (dp_index // 2 * mp_size + mp_index) % side

    def send(value, row_step, column_step, flip):
        return lax.ppermute(value, AXES, layout.permutation(row_step, column_step, flip))

    scalars = jnp.concatenate([jnp.exp(log_scale), logit_bias])
    images, texts = [image_feats], [text_feats]
    for t in range(1, side):
        images.append(send(image_feats, 0, t, 0))
        texts.append(send(text_feats, t, 0, 0))
    image_shards = [y for x in images for y in (x, send(x, 0, 0, 1))]
    text_shards = [y for x in texts for y in (x, send(x, 0, 0, 1))]

    own, *messages, stats = block_grads(
        layout, scalars, image_proj, text_proj, image_shards, text_shards
    )
    all_stats = lax.all_gather(stats, AXES, axis=0)
    for t in range(1, side):
        own = own + send(messages[t - 1], t, 0, 0).astype(F32)

    blocks = own.reshape(side // mp_size, 2, mp_size, out_rows, width)

    def piece(column, role):
        start = (column // mp_size, role, column % mp_size, 0, 0)
        return lax.dynamic_slice(blocks, start, (1, 1, 1, out_rows, width))[0, 0, 0]

    sums = []
    for flip in range(2):
        total = None
        for t in range(side):
            part = piece((unit_column + t) % side, core ^ flip)
            if t or flip:
                part = send(part.astype(BF16), 0, t, flip).astype(F32)
            total = part if total is None else total + part
        sums.append(total)
    same, other = sums
    image_proj_grad = jnp.where(core == 0, same, other)
    text_proj_grad = jnp.where(core == 0, other, same)
    totals = jnp.sum(all_stats, axis=(0, 2)) * (0.5 / batch_total)
    return totals[0:1], image_proj_grad, text_proj_grad, totals[1:2], totals[2:3]


def solution(mesh):
    layout = Layout(mesh.shape["dp"], mesh.shape["mp"])
    return jax.shard_map(
        functools.partial(per_device, layout),
        mesh=mesh,
        in_specs=(P(AXES, None), P(AXES, None), P(), P(), P(), P()),
        out_specs=(P(), P(AXES, None), P(AXES, None), P(), P()),
        check_vma=False,
    )
```

```python
import functools
import math

import jax
import jax.numpy as jnp
from jax import lax
from jax.experimental import pallas as pl
from jax.experimental.pallas import tpu as pltpu
from jax.sharding import PartitionSpec as P

F32 = jnp.float32
BF16 = jnp.bfloat16
AXES = ("dp", "mp")


class Layout:
    def __init__(self, dp_size, mp_size):
        self.dp, self.mp = dp_size, mp_size
        self.units = dp_size * mp_size // 2
        self.side = math.isqrt(self.units)
        if self.side * self.side != self.units or self.side % mp_size or self.side & (self.side - 1):
            raise ValueError("unsupported mesh")

    def device(self, unit, core):
        return (2 * (unit // self.mp) + core) * self.mp + unit % self.mp

    def send(self, value, step):
        s = self.side
        pairs = []
        for unit in range(self.units):
            for core in range(2):
                row, column, other = step(*divmod(unit, s), core)
                pairs.append((self.device(unit, core), self.device(row * s + column, other)))
        return lax.ppermute(value, AXES, pairs)

    def along_column(self, value, t):
        return self.send(value, lambda r, c, core: (r ^ t, c, core))

    def along_row(self, value, t):
        return self.send(value, lambda r, c, core: (r, c ^ t, core))

    def along_role(self, value, t):
        return self.send(value, lambda r, c, core: (r ^ t, c, 1) if core else (r, c ^ t, 0))

    def sibling(self, value):
        return self.send(value, lambda r, c, core: (r, c, 1 - core))


def tree_sum(values):
    values = list(values)
    while len(values) > 1:
        values = [a + b for a, b in zip(values[::2], values[1::2])]
    return values[0]


def load_projections(image_proj, text_proj, projs, sems):
    core = lax.rem(lax.axis_index("dp"), 2)
    own = pltpu.make_async_copy(image_proj, projs.at[core], sems.at[0])
    other = pltpu.make_async_copy(text_proj, projs.at[1 - core], sems.at[1])
    own.start()
    other.start()
    return own, other


def project(rows, projection):
    raw = jnp.dot(rows, projection, preferred_element_type=F32)
    inverse = lax.rsqrt(jnp.sum(raw * raw, axis=-1, keepdims=True) + 1e-06)
    return raw * inverse, inverse


def project_kernel(image_proj, text_proj, own, other, own_unit, own_inverse, other_half, projs, sems):
    for copy in load_projections(image_proj, text_proj, projs, sems):
        copy.wait()
    unit, _ = project(other[...], projs[1])
    other_half[...] = unit.astype(BF16)
    unit, inverse = project(own[...], projs[0])
    own_unit[...] = unit
    own_inverse[...] = jnp.broadcast_to(inverse, own_inverse.shape)


def project_chunks(image_proj, text_proj, own, other):
    rows, width = own.shape
    anywhere = pl.BlockSpec(memory_space=pl.ANY)
    vmem = pl.BlockSpec(memory_space=pltpu.VMEM)
    return pl.pallas_call(
        project_kernel,
        out_shape=[
            jax.ShapeDtypeStruct((rows, width), F32),
            jax.ShapeDtypeStruct((rows, 128), F32),
            jax.ShapeDtypeStruct((rows, width), BF16),
        ],
        in_specs=[anywhere] * 2 + [vmem] * 2,
        out_specs=[vmem] * 3,
        scratch_shapes=[pltpu.VMEM((2, width, width), BF16), pltpu.SemaphoreType.DMA((2,))],
        compiler_params=pltpu.CompilerParams(vmem_limit_bytes=20 * 1024 * 1024),
        cost_estimate=pl.CostEstimate(
            flops=4 * rows * width * width,
            bytes_accessed=4 * width * width + 10 * rows * width,
            transcendentals=2 * rows,
        ),
        name="project",
    )(image_proj, text_proj, own, other)


def pair_terms(cosine, scale, bias, masked):
    logits = scale * cosine + bias
    small = jnp.exp(-jnp.abs(logits))
    inverse_sum = 1.0 / (1.0 + small)
    large_side = logits >= 0.0
    pair_grads = jnp.where(large_side, inverse_sum, small * inverse_sum)
    tops = jnp.maximum(logits, 0.0)
    if masked:
        equal = lax.broadcasted_iota(jnp.int32, cosine.shape, 0) == lax.broadcasted_iota(
            jnp.int32, cosine.shape, 1
        )
        lower = jnp.where(large_side, small * inverse_sum, inverse_sum)
        pair_grads = jnp.where(equal, -lower, pair_grads)
        tops = jnp.where(equal, jnp.maximum(-logits, 0.0), tops)
    return tops + jnp.log1p(small), pair_grads


def lane_sums(values):
    total = jnp.sum(values, axis=0, keepdims=True)
    return sum(total[:, j : j + 128] for j in range(0, total.shape[1], 128))


def block_kernel(side, mp_size, first_width, scalars, image_proj, text_proj, *refs):
    own_chunks, refs = refs[:side], refs[side:]
    last_other, refs = refs[0], refs[1:]
    own_units, refs = refs[: side - 1], refs[side - 1 :]
    own_inverses, refs = refs[: side - 1], refs[side - 1 :]
    other_halves, refs = refs[: side - 1], refs[side - 1 :]
    firsts, refs = refs[:side], refs[side:]
    lates, refs = refs[:side], refs[side:]
    stats, projs, last, feats, units, inverses, other_half, dy, grad, piece, sems = refs
    rows, width = dy.shape
    chunk_rows = rows // side
    rest = rows - chunk_rows
    dp_index, mp_index = lax.axis_index("dp"), lax.axis_index("mp")
    unit_index = dp_index // 2 * mp_size + mp_index
    unit_row, unit_column = unit_index // side, lax.rem(unit_index, side)
    scale, bias = scalars[0], scalars[1]

    count = 2

    def start(source, target):
        nonlocal count
        copy = pltpu.make_async_copy(source, target, sems.at[count])
        copy.start()
        count += 1
        return copy

    def places(i):
        return pl.ds(i * chunk_rows, chunk_rows)

    last_copy = start(last_other, last)
    own_copies = [start(own_chunks[side - 1], feats.at[places(side - 1)])]
    proj_copies = load_projections(image_proj, text_proj, projs, sems)
    other_copies = [start(other_halves[i], other_half.at[places(i)]) for i in range(side - 1)]
    unit_copies = [start(own_units[i], units.at[places(i)]) for i in range(side - 1)]
    unit_copies += [start(own_inverses[i], inverses.at[places(i)]) for i in range(side - 1)]
    feat_copies = [start(own_chunks[i], feats.at[places(i)]) for i in range(side - 1)]

    for copy in [last_copy, *own_copies, *proj_copies]:
        copy.wait()
    unit, _ = project(last[...], projs[1])
    other_half[rest:, :] = unit.astype(BF16)
    unit, inverse = project(feats[rest:, :], projs[0])
    units[rest:, :] = unit
    inverses[rest:, :] = jnp.broadcast_to(inverse, (chunk_rows, 128))
    for copy in other_copies + unit_copies:
        copy.wait()

    def tile(place, with_partners):
        unit = units[place, :]
        cosine = lax.dot_general(
            unit.astype(BF16), other_half[...], (((1,), (1,)), ((), ())), preferred_element_type=F32
        )
        if with_partners:
            terms = [
                pair_terms(cosine[:, :chunk_rows], scale, bias, True),
                pair_terms(cosine[:, chunk_rows:], scale, bias, False),
            ]
            losses, pair_grads = [jnp.concatenate(x, axis=1) for x in zip(*terms)]
        else:
            losses, pair_grads = pair_terms(cosine, scale, bias, False)
        half_grads = pair_grads.astype(BF16)
        sums = jnp.concatenate(
            [lane_sums(losses), lane_sums(pair_grads * cosine) * scale, lane_sums(pair_grads)], axis=1
        )
        stats[0:1, :] = sums if with_partners else stats[0:1, :] + sums
        inner = jnp.sum(half_grads.astype(F32) * cosine, axis=-1, keepdims=True)
        grads = jnp.dot(half_grads, other_half[...], preferred_element_type=F32)
        dy[place, :] = ((grads - unit * inner) * (scale * inverses[place, 0:1])).astype(BF16)

    tile(pl.ds(0, chunk_rows), True)

    @pl.loop(1, side)
    def _(i):
        tile(pl.ds(pl.multiple_of(i * chunk_rows, chunk_rows), chunk_rows), False)

    for copy in feat_copies:
        copy.wait()
    for j in range(0, width, 128):
        grad[j : j + 128, :] = lax.dot_general(
            feats[:, j : j + 128], dy[...], (((0,), (0,)), ((), ())), preferred_element_type=F32
        )

    sums = stats[0:1, :]
    stats[...] = jnp.broadcast_to(sums, stats.shape)
    chunk = width // side
    for t in range(side):
        first = pl.multiple_of(jnp.bitwise_xor(unit_row, t) * chunk, chunk)
        firsts[t][:chunk, :] = grad[pl.ds(first, chunk), :first_width].astype(firsts[t].dtype)
        if t:
            firsts[t][chunk:, :] = stat_rows(sums, first_width).astype(BF16)

    out_rows = chunk // (2 * side)
    for column in range(side):
        for i in range(side):
            for core in range(2):
                source = i * chunk + shard_of(column, core, mp_size) * out_rows
                target = (2 * i + core) * out_rows
                piece[target : target + out_rows, :] = grad[source : source + out_rows, first_width:]
        store_for(column, unit_column, piece, lates)


def shard_of(column, core, mp_size):
    return column // mp_size * 2 * mp_size + core * mp_size + column % mp_size


def store_for(index, own_index, piece, outs):
    for t, out in enumerate(outs):

        @pl.when(jnp.bitwise_xor(own_index, t) == index)
        def _():
            out[...] = piece[...].astype(out.dtype)


def stat_rows(sums, width):
    part0 = sums.astype(BF16).astype(F32)
    part1 = (sums - part0).astype(BF16).astype(F32)
    part2 = sums - part0 - part1
    line = lax.broadcasted_iota(jnp.int32, (8, sums.shape[1]), 0)
    parts = jnp.where(line == 0, part0, jnp.where(line == 1, part1, jnp.where(line == 2, part2, 0.0)))
    if width > sums.shape[1]:
        parts = jnp.concatenate([parts, jnp.zeros((8, width - sums.shape[1]), F32)], axis=1)
    return parts


def block_grads(
    layout, first_width, scalars, image_proj, text_proj, own_chunks, last_other, projected
):
    side = layout.side
    chunk_rows, width = own_chunks[0].shape
    rows = side * chunk_rows
    chunk = width // side
    anywhere = pl.BlockSpec(memory_space=pl.ANY)
    vmem = pl.BlockSpec(memory_space=pltpu.VMEM)
    late_width = width - first_width
    operands = [image_proj, text_proj, *own_chunks, last_other]
    operands += [x for column in zip(*projected) for x in column]
    return pl.pallas_call(
        functools.partial(block_kernel, side, layout.mp, first_width),
        out_shape=[jax.ShapeDtypeStruct((chunk, first_width), F32)]
        + [jax.ShapeDtypeStruct((chunk + 8, first_width), BF16)] * (side - 1)
        + [jax.ShapeDtypeStruct((chunk, late_width), F32)]
        + [jax.ShapeDtypeStruct((chunk, late_width), BF16)] * (side - 1)
        + [jax.ShapeDtypeStruct((8, 384), F32)],
        in_specs=[pl.BlockSpec(memory_space=pltpu.SMEM)] + [anywhere] * len(operands),
        out_specs=[vmem] * (2 * side + 1),
        scratch_shapes=[
            pltpu.VMEM((2, width, width), BF16),
            pltpu.VMEM((chunk_rows, width), BF16),
            pltpu.VMEM((rows, width), BF16),
            pltpu.VMEM((rows, width), F32),
            pltpu.VMEM((rows, 128), F32),
            pltpu.VMEM((rows, width), BF16),
            pltpu.VMEM((rows, width), BF16),
            pltpu.VMEM((width, width), F32),
            pltpu.VMEM((chunk, late_width), F32),
            pltpu.SemaphoreType.DMA((len(operands),)),
        ],
        compiler_params=pltpu.CompilerParams(vmem_limit_bytes=56 * 1024 * 1024),
        cost_estimate=pl.CostEstimate(
            flops=2 * rows * width * (2 * rows + width) + 4 * chunk_rows * width * width,
            bytes_accessed=8 * rows * width + 8 * width * width,
            transcendentals=3 * rows * rows,
        ),
        name="block",
    )(scalars, *operands)


def arrived_sum(own, arrived, rows):
    return tree_sum([own[:rows, :]] + [x[:rows, :].astype(F32) for x in arrived])


def first_kernel(side, mp_size, own, own_stats, *refs):
    arrived, outs = refs[: side - 1], refs[side - 1 : 2 * side - 1]
    stats, total, piece = refs[2 * side - 1 :]
    chunk, width = own.shape
    out_rows = chunk // (2 * side)
    total[...] = arrived_sum(own, arrived, chunk)
    parts = [x[chunk:, :384].astype(F32) for x in arrived]
    sums = tree_sum([own_stats[0:1, :]] + [x[0:1] + x[1:2] + x[2:3] for x in parts])
    stats[...] = jnp.broadcast_to(sums, stats.shape)
    dp_index, mp_index = lax.axis_index("dp"), lax.axis_index("mp")
    unit_column = lax.rem(dp_index // 2 * mp_size + mp_index, side)
    piece[2 * out_rows :, :] = jnp.zeros((piece.shape[0] - 2 * out_rows, width), F32)
    piece[piece.shape[0] - 8 :, :] = stat_rows(sums, width)
    for column in range(side):
        for core in range(2):
            source = shard_of(column, core, mp_size) * out_rows
            piece[core * out_rows : (core + 1) * out_rows, :] = total[source : source + out_rows, :]
        store_for(column, unit_column, piece, outs)


def first_pieces(layout, own, own_stats, arrived):
    side = layout.side
    chunk, width = own.shape
    rows = (2 * (chunk // (2 * side)) + 7) // 8 * 8 + 8
    vmem = pl.BlockSpec(memory_space=pltpu.VMEM)
    return pl.pallas_call(
        functools.partial(first_kernel, side, layout.mp),
        out_shape=[jax.ShapeDtypeStruct((rows, width), F32)]
        + [jax.ShapeDtypeStruct((rows, width), BF16)] * (side - 1)
        + [jax.ShapeDtypeStruct((8, 384), F32)],
        in_specs=[vmem] * (side + 1),
        out_specs=[vmem] * (side + 1),
        scratch_shapes=[pltpu.VMEM((chunk, width), F32), pltpu.VMEM((rows, width), F32)],
        compiler_params=pltpu.CompilerParams(vmem_limit_bytes=12 * 1024 * 1024),
        name="first",
    )(own, own_stats, *arrived)


def late_kernel(side, mp_size, own, *refs):
    arrived, outs, total = refs[: side - 1], refs[side - 1 : 2 * side - 1], refs[-1]
    chunk = own.shape[0]
    total[...] = arrived_sum(own, arrived, chunk)
    dp_index, mp_index = lax.axis_index("dp"), lax.axis_index("mp")
    unit_row = (dp_index // 2 * mp_size + mp_index) // side
    rows = chunk // side
    for row in range(side):
        store_for(row, unit_row, total.at[row * rows : (row + 1) * rows, :], outs)


def late_pieces(layout, own, arrived):
    side = layout.side
    chunk, width = own.shape
    rows = chunk // side
    vmem = pl.BlockSpec(memory_space=pltpu.VMEM)
    return pl.pallas_call(
        functools.partial(late_kernel, side, layout.mp),
        out_shape=[jax.ShapeDtypeStruct((rows, width), F32)]
        + [jax.ShapeDtypeStruct((rows, width), BF16)] * (side - 1),
        in_specs=[vmem] * side,
        out_specs=[vmem] * side,
        scratch_shapes=[pltpu.VMEM((chunk, width), F32)],
        compiler_params=pltpu.CompilerParams(vmem_limit_bytes=12 * 1024 * 1024),
        name="late",
    )(own, *arrived)


def per_device(layout, image_feats, text_feats, image_proj, text_proj, log_scale, logit_bias):
    side = layout.side
    own_rows, width = image_feats.shape
    devices = layout.dp * layout.mp
    out_rows = width // devices
    batch_total = own_rows * devices
    is_image = lax.axis_index("dp") % 2 == 0

    scalars = jnp.concatenate([jnp.exp(log_scale), logit_bias])
    sibling_image, sibling_text = layout.sibling(image_feats), layout.sibling(text_feats)
    own_unit = jnp.concatenate(
        [jnp.where(is_image, image_feats, sibling_text), jnp.where(is_image, sibling_image, text_feats)]
    )
    other_unit = jnp.concatenate(
        [jnp.where(is_image, text_feats, sibling_image), jnp.where(is_image, sibling_text, image_feats)]
    )
    own_chunks, other_chunks = {0: own_unit}, {0: other_unit}
    bit = side // 2
    projected = {}
    while bit:
        sources = list(own_chunks)
        if bit == 1:
            own_chunks[1] = layout.along_role(own_unit, 1)
            projected[0] = project_chunks(image_proj, text_proj, own_unit, other_unit)
            own_chunks, projected = lax.optimization_barrier((own_chunks, projected))
        for t in sources:
            if t ^ bit not in own_chunks:
                own_chunks[t ^ bit] = layout.along_role(own_chunks[t], bit)
        bit //= 2
    last = side - 1
    for t in range(1, last):
        other_chunks[t] = layout.sibling(own_chunks[t])
        projected[t] = project_chunks(image_proj, text_proj, own_chunks[t], other_chunks[t])
    own_chunks[last], projected = lax.optimization_barrier((own_chunks[last], projected))
    other_chunks[last] = layout.sibling(own_chunks[last])
    first_width = width - width // 3
    results = block_grads(
        layout,
        first_width,
        scalars,
        image_proj,
        text_proj,
        [own_chunks[t] for t in range(side)],
        other_chunks[last],
        [projected[t] for t in range(last)],
    )
    firsts, lates, stats = list(results[:side]), list(results[side : 2 * side]), results[-1]

    firsts[1:] = [layout.along_column(firsts[t], t) for t in range(1, side)]
    lates[1:] = [layout.along_row(lates[t], t) for t in range(1, side)]
    *firsts, stats = first_pieces(layout, firsts[0], stats, firsts[1:])
    lates = list(late_pieces(layout, lates[0], lates[1:]))

    firsts[1:] = [layout.along_row(firsts[t], t) for t in range(1, side)]
    lates[1:] = [layout.along_column(lates[t], t) for t in range(1, side)]
    last_rows = 2 * out_rows
    first_sum = tree_sum([x[:last_rows].astype(F32) for x in firsts])
    late_sum = tree_sum([x.astype(F32) for x in lates])
    total = jnp.concatenate([first_sum, late_sum], axis=1)
    parts = [x[-8:-5, :384].astype(F32) for x in firsts[1:]]
    stat_total = tree_sum([stats[0]] + [x[0] + x[1] + x[2] for x in parts])

    upper, lower = total[:out_rows], total[out_rows:]
    keep, give = jnp.where(is_image, upper, lower), jnp.where(is_image, lower, upper)
    got = layout.sibling(give)
    image_proj_grad = jnp.where(is_image, keep, got)
    text_proj_grad = jnp.where(is_image, got, keep)
    stat_total = stat_total + layout.sibling(stat_total)
    totals = jnp.sum(stat_total.reshape(3, 128), axis=1) * (0.5 / batch_total)
    return totals[0:1], image_proj_grad, text_proj_grad, totals[1:2], totals[2:3]


def solution(mesh):
    layout = Layout(mesh.shape["dp"], mesh.shape["mp"])
    return jax.shard_map(
        functools.partial(per_device, layout),
        mesh=mesh,
        in_specs=(P(AXES, None), P(AXES, None), P(), P(), P(), P()),
        out_specs=(P(), P(AXES, None), P(AXES, None), P(), P()),
        check_vma=False,
    )
```

```python
import functools
import math

import jax
import jax.numpy as jnp
from jax import lax
from jax.experimental import pallas as pl
from jax.experimental.pallas import tpu as pltpu
from jax.sharding import PartitionSpec as P

F32 = jnp.float32
BF16 = jnp.bfloat16
AXES = ("dp", "mp")


class Layout:
    def __init__(self, dp_size, mp_size):
        self.dp, self.mp = dp_size, mp_size
        self.units = dp_size * mp_size // 2
        self.side = math.isqrt(self.units)
        if self.side * self.side != self.units or self.side % mp_size or self.side & (self.side - 1):
            raise ValueError("unsupported mesh")

    def device(self, unit, core):
        return (2 * (unit // self.mp) + core) * self.mp + unit % self.mp

    def send(self, value, step):
        s = self.side
        pairs = []
        for unit in range(self.units):
            for core in range(2):
                row, column, other = step(*divmod(unit, s), core)
                pairs.append((self.device(unit, core), self.device(row * s + column, other)))
        return lax.ppermute(value, AXES, pairs)

    def along_column(self, value, t):
        return self.send(value, lambda r, c, core: (r ^ t, c, core))

    def along_row(self, value, t):
        return self.send(value, lambda r, c, core: (r, c ^ t, core))

    def sibling(self, value):
        return self.send(value, lambda r, c, core: (r, c, 1 - core))


def tree_sum(values):
    values = list(values)
    while len(values) > 1:
        values = [a + b for a, b in zip(values[::2], values[1::2])]
    return values[0]


def this_core():
    return lax.rem(lax.axis_index("dp"), 2)


def load_projections(image_proj, text_proj, projs, sems):
    core = this_core()
    own = pltpu.make_async_copy(image_proj, projs.at[core], sems.at[0])
    other = pltpu.make_async_copy(text_proj, projs.at[1 - core], sems.at[1])
    own.start()
    other.start()
    return [own, other]


def load_chunk(shards, feats, sems):
    core = this_core()
    rows = shards[0].shape[0]
    copies = []
    for i, shard in enumerate(shards):
        place = pl.ds((core if i < 2 else 1 - core) * rows, rows)
        side = core if i % 2 == 0 else 1 - core
        copies.append(pltpu.make_async_copy(shard, feats.at[side, place], sems.at[i]))
        copies[-1].start()
    return copies


def project(rows, projection):
    raw = jnp.dot(rows, projection, preferred_element_type=F32)
    inverse = lax.rsqrt(jnp.sum(raw * raw, axis=-1, keepdims=True) + 1e-06)
    return raw * inverse, inverse


def project_kernel(image_proj, text_proj, *refs):
    shards, (own_chunk, own_unit, own_inverse, other_half, feats, projs, sems) = refs[:4], refs[4:]
    copies = load_chunk(shards, feats, sems.at[pl.ds(2, 4)])
    copies += load_projections(image_proj, text_proj, projs, sems.at[pl.ds(0, 2)])
    for copy in copies:
        copy.wait()
    unit, _ = project(feats[1], projs[1])
    other_half[...] = unit.astype(BF16)
    unit, inverse = project(feats[0], projs[0])
    own_unit[...] = unit
    own_inverse[...] = jnp.broadcast_to(inverse, own_inverse.shape)
    own_chunk[...] = feats[0]


def project_chunk(image_proj, text_proj, shards):
    rows, width = shards[0].shape
    rows = 2 * rows
    anywhere = pl.BlockSpec(memory_space=pl.ANY)
    vmem = pl.BlockSpec(memory_space=pltpu.VMEM)
    return pl.pallas_call(
        project_kernel,
        out_shape=[
            jax.ShapeDtypeStruct((rows, width), BF16),
            jax.ShapeDtypeStruct((rows, width), F32),
            jax.ShapeDtypeStruct((rows, 128), F32),
            jax.ShapeDtypeStruct((rows, width), BF16),
        ],
        in_specs=[anywhere] * 6,
        out_specs=[vmem] * 4,
        scratch_shapes=[
            pltpu.VMEM((2, rows, width), BF16),
            pltpu.VMEM((2, width, width), BF16),
            pltpu.SemaphoreType.DMA((6,)),
        ],
        compiler_params=pltpu.CompilerParams(
            vmem_limit_bytes=4 * width * width + 24 * rows * width + 4 * 1024 * 1024
        ),
        cost_estimate=pl.CostEstimate(
            flops=4 * rows * width * width,
            bytes_accessed=4 * width * width + 12 * rows * width,
            transcendentals=2 * rows,
        ),
        name="project",
    )(image_proj, text_proj, *shards)


def pair_terms(cosine, scale, bias, masked):
    logits = scale * cosine + bias
    small = jnp.exp(-jnp.abs(logits))
    inverse_sum = 1.0 / (1.0 + small)
    large_side = logits >= 0.0
    pair_grads = jnp.where(large_side, inverse_sum, small * inverse_sum)
    tops = jnp.maximum(logits, 0.0)
    if masked:
        equal = lax.broadcasted_iota(jnp.int32, cosine.shape, 0) == lax.broadcasted_iota(
            jnp.int32, cosine.shape, 1
        )
        lower = jnp.where(large_side, small * inverse_sum, inverse_sum)
        pair_grads = jnp.where(equal, -lower, pair_grads)
        tops = jnp.where(equal, jnp.maximum(-logits, 0.0), tops)
    return tops + jnp.log1p(small), pair_grads


def lane_sums(values):
    total = jnp.sum(values, axis=0, keepdims=True)
    return sum(total[:, j : j + 128] for j in range(0, total.shape[1], 128))


def block_kernel(side, mp_size, first_width, scalars, image_proj, text_proj, *refs):
    last_shards, refs = refs[:4], refs[4:]
    own_chunks, refs = refs[: side - 1], refs[side - 1 :]
    own_units, refs = refs[: side - 1], refs[side - 1 :]
    own_inverses, refs = refs[: side - 1], refs[side - 1 :]
    other_halves, refs = refs[: side - 1], refs[side - 1 :]
    firsts, refs = refs[:side], refs[side:]
    lates, refs = refs[:side], refs[side:]
    stats, projs, last, feats, units, inverses, other_half, dy, grad, piece, sems = refs
    rows, width = dy.shape
    chunk_rows = rows // side
    rest = rows - chunk_rows
    dp_index, mp_index = lax.axis_index("dp"), lax.axis_index("mp")
    unit_index = dp_index // 2 * mp_size + mp_index
    unit_row, unit_column = unit_index // side, lax.rem(unit_index, side)
    scale, bias = scalars[0], scalars[1]

    count = 6

    def start(source, target):
        nonlocal count
        copy = pltpu.make_async_copy(source, target, sems.at[count])
        copy.start()
        count += 1
        return copy

    def places(i):
        return pl.ds(i * chunk_rows, chunk_rows)

    first_copies = load_chunk(last_shards, last, sems.at[pl.ds(2, 4)])
    first_copies += load_projections(image_proj, text_proj, projs, sems.at[pl.ds(0, 2)])
    other_copies = [start(other_halves[i], other_half.at[places(i)]) for i in range(side - 1)]
    unit_copies = [start(own_units[i], units.at[places(i)]) for i in range(side - 1)]
    unit_copies += [start(own_inverses[i], inverses.at[places(i)]) for i in range(side - 1)]
    feat_copies = [start(own_chunks[i], feats.at[places(i)]) for i in range(side - 1)]

    for copy in first_copies:
        copy.wait()
    unit, _ = project(last[1], projs[1])
    other_half[rest:, :] = unit.astype(BF16)
    unit, inverse = project(last[0], projs[0])
    units[rest:, :] = unit
    inverses[rest:, :] = jnp.broadcast_to(inverse, (chunk_rows, 128))
    feats[rest:, :] = last[0]
    for copy in other_copies + unit_copies:
        copy.wait()

    def tile(place, with_partners):
        unit = units[place, :]
        cosine = lax.dot_general(
            unit.astype(BF16), other_half[...], (((1,), (1,)), ((), ())), preferred_element_type=F32
        )
        if with_partners:
            terms = [
                pair_terms(cosine[:, :chunk_rows], scale, bias, True),
                pair_terms(cosine[:, chunk_rows:], scale, bias, False),
            ]
            losses, pair_grads = [jnp.concatenate(x, axis=1) for x in zip(*terms)]
        else:
            losses, pair_grads = pair_terms(cosine, scale, bias, False)
        half_grads = pair_grads.astype(BF16)
        sums = jnp.concatenate(
            [lane_sums(losses), lane_sums(pair_grads * cosine) * scale, lane_sums(pair_grads)], axis=1
        )
        stats[0:1, :] = sums if with_partners else stats[0:1, :] + sums
        inner = jnp.sum(half_grads.astype(F32) * cosine, axis=-1, keepdims=True)
        grads = jnp.dot(half_grads, other_half[...], preferred_element_type=F32)
        dy[place, :] = ((grads - unit * inner) * (scale * inverses[place, 0:1])).astype(BF16)

    tile(pl.ds(0, chunk_rows), True)

    @pl.loop(1, side)
    def _(i):
        tile(pl.ds(pl.multiple_of(i * chunk_rows, chunk_rows), chunk_rows), False)

    for copy in feat_copies:
        copy.wait()
    for j in range(0, width, 128):
        grad[j : j + 128, :] = lax.dot_general(
            feats[:, j : j + 128], dy[...], (((0,), (0,)), ((), ())), preferred_element_type=F32
        )

    sums = stats[0:1, :]
    stats[...] = jnp.broadcast_to(sums, stats.shape)
    chunk = width // side
    for t in range(side):
        first = pl.multiple_of(jnp.bitwise_xor(unit_row, t) * chunk, chunk)
        firsts[t][:chunk, :] = grad[pl.ds(first, chunk), :first_width].astype(firsts[t].dtype)
        if t:
            firsts[t][chunk:, :] = stat_rows(sums, first_width).astype(BF16)
    out_rows = chunk // (2 * side)
    for column in range(side):
        for i in range(side):
            for core in range(2):
                source = i * chunk + shard_of(column, core, mp_size) * out_rows
                target = (2 * i + core) * out_rows
                piece[target : target + out_rows, :] = grad[source : source + out_rows, first_width:]
        store_for(column, unit_column, piece, lates)


def shard_of(column, core, mp_size):
    return column // mp_size * 2 * mp_size + core * mp_size + column % mp_size


def store_for(index, own_index, piece, outs):
    for t, out in enumerate(outs):

        @pl.when(jnp.bitwise_xor(own_index, t) == index)
        def _():
            out[...] = piece[...].astype(out.dtype)


def stat_rows(sums, width):
    part0 = sums.astype(BF16).astype(F32)
    part1 = (sums - part0).astype(BF16).astype(F32)
    part2 = sums - part0 - part1
    line = lax.broadcasted_iota(jnp.int32, (8, sums.shape[1]), 0)
    parts = jnp.where(line == 0, part0, jnp.where(line == 1, part1, jnp.where(line == 2, part2, 0.0)))
    if width > sums.shape[1]:
        parts = jnp.concatenate([parts, jnp.zeros((8, width - sums.shape[1]), F32)], axis=1)
    return parts


def block_grads(layout, first_width, scalars, image_proj, text_proj, last_shards, projected):
    side = layout.side
    chunk_rows, width = projected[0][0].shape
    rows = side * chunk_rows
    chunk = width // side
    anywhere = pl.BlockSpec(memory_space=pl.ANY)
    vmem = pl.BlockSpec(memory_space=pltpu.VMEM)
    late_width = width - first_width
    operands = [image_proj, text_proj, *last_shards]
    operands += [x for column in zip(*projected) for x in column]
    needed = 4 * width * width + 12 * rows * width + 4 * chunk_rows * width
    needed += 4 * width * (width + late_width) + 24 * chunk_rows * rows + 14 * 1024 * 1024
    return pl.pallas_call(
        functools.partial(block_kernel, side, layout.mp, first_width),
        out_shape=[jax.ShapeDtypeStruct((chunk, first_width), F32)]
        + [jax.ShapeDtypeStruct((chunk + 8, first_width), BF16)] * (side - 1)
        + [jax.ShapeDtypeStruct((chunk, late_width), F32)]
        + [jax.ShapeDtypeStruct((chunk, late_width), BF16)] * (side - 1)
        + [jax.ShapeDtypeStruct((8, 384), F32)],
        in_specs=[pl.BlockSpec(memory_space=pltpu.SMEM)] + [anywhere] * len(operands),
        out_specs=[vmem] * (2 * side + 1),
        scratch_shapes=[
            pltpu.VMEM((2, width, width), BF16),
            pltpu.VMEM((2, chunk_rows, width), BF16),
            pltpu.VMEM((rows, width), BF16),
            pltpu.VMEM((rows, width), F32),
            pltpu.VMEM((rows, 128), F32),
            pltpu.VMEM((rows, width), BF16),
            pltpu.VMEM((rows, width), BF16),
            pltpu.VMEM((width, width), F32),
            pltpu.VMEM((chunk, late_width), F32),
            pltpu.SemaphoreType.DMA((len(operands),)),
        ],
        compiler_params=pltpu.CompilerParams(vmem_limit_bytes=min(needed, 60 * 1024 * 1024)),
        cost_estimate=pl.CostEstimate(
            flops=2 * rows * width * (2 * rows + width) + 4 * chunk_rows * width * width,
            bytes_accessed=12 * rows * width + 4 * width * width,
            transcendentals=3 * rows * rows,
        ),
        name="block",
    )(scalars, *operands)


def arrived_sum(own, arrived, rows):
    return tree_sum([own[:rows, :]] + [x[:rows, :].astype(F32) for x in arrived])


def first_kernel(side, mp_size, own, own_stats, *refs):
    arrived, outs = refs[: side - 1], refs[side - 1 : 2 * side - 1]
    stats, total, piece = refs[2 * side - 1 :]
    chunk, width = own.shape
    out_rows = chunk // (2 * side)
    total[...] = arrived_sum(own, arrived, chunk)
    parts = [x[chunk:, :384].astype(F32) for x in arrived]
    sums = tree_sum([own_stats[0:1, :]] + [x[0:1] + x[1:2] + x[2:3] for x in parts])
    stats[...] = jnp.broadcast_to(sums, stats.shape)
    dp_index, mp_index = lax.axis_index("dp"), lax.axis_index("mp")
    unit_column = lax.rem(dp_index // 2 * mp_size + mp_index, side)
    piece[2 * out_rows :, :] = jnp.zeros((piece.shape[0] - 2 * out_rows, width), F32)
    piece[piece.shape[0] - 8 :, :] = stat_rows(sums, width)
    for column in range(side):
        for core in range(2):
            source = shard_of(column, core, mp_size) * out_rows
            piece[core * out_rows : (core + 1) * out_rows, :] = total[source : source + out_rows, :]
        store_for(column, unit_column, piece, outs)


def first_pieces(layout, own, own_stats, arrived):
    side = layout.side
    chunk, width = own.shape
    rows = (2 * (chunk // (2 * side)) + 7) // 8 * 8 + 8
    vmem = pl.BlockSpec(memory_space=pltpu.VMEM)
    return pl.pallas_call(
        functools.partial(first_kernel, side, layout.mp),
        out_shape=[jax.ShapeDtypeStruct((rows, width), F32)]
        + [jax.ShapeDtypeStruct((rows, width), BF16)] * (side - 1)
        + [jax.ShapeDtypeStruct((8, 384), F32)],
        in_specs=[vmem] * (side + 1),
        out_specs=[vmem] * (side + 1),
        scratch_shapes=[pltpu.VMEM((chunk, width), F32), pltpu.VMEM((rows, width), F32)],
        compiler_params=pltpu.CompilerParams(vmem_limit_bytes=12 * 1024 * 1024),
        name="first",
    )(own, own_stats, *arrived)


def late_kernel(side, mp_size, own, *refs):
    arrived, outs, total = refs[: side - 1], refs[side - 1 : 2 * side - 1], refs[-1]
    chunk = own.shape[0]
    total[...] = arrived_sum(own, arrived, chunk)
    dp_index, mp_index = lax.axis_index("dp"), lax.axis_index("mp")
    unit_row = (dp_index // 2 * mp_size + mp_index) // side
    rows = chunk // side
    for row in range(side):
        store_for(row, unit_row, total.at[row * rows : (row + 1) * rows, :], outs)


def late_pieces(layout, own, arrived):
    side = layout.side
    chunk, width = own.shape
    rows = chunk // side
    vmem = pl.BlockSpec(memory_space=pltpu.VMEM)
    return pl.pallas_call(
        functools.partial(late_kernel, side, layout.mp),
        out_shape=[jax.ShapeDtypeStruct((rows, width), F32)]
        + [jax.ShapeDtypeStruct((rows, width), BF16)] * (side - 1),
        in_specs=[vmem] * side,
        out_specs=[vmem] * side,
        scratch_shapes=[pltpu.VMEM((chunk, width), F32)],
        compiler_params=pltpu.CompilerParams(vmem_limit_bytes=12 * 1024 * 1024),
        name="late",
    )(own, *arrived)


def per_device(layout, image_feats, text_feats, image_proj, text_proj, log_scale, logit_bias):
    side = layout.side
    own_rows, width = image_feats.shape
    devices = layout.dp * layout.mp
    out_rows = width // devices
    batch_total = own_rows * devices
    is_image = lax.axis_index("dp") % 2 == 0

    scalars = jnp.concatenate([jnp.exp(log_scale), logit_bias])

    images, texts, swapped, projected = {0: image_feats}, {0: text_feats}, {}, {}

    def swap(t):
        swapped[t] = layout.sibling(images[t]), layout.sibling(texts[t])

    def project_next(t):
        projected[t] = project_chunk(image_proj, text_proj, [images[t], texts[t], *swapped[t]])

    last = side - 1
    bit = side // 2
    while bit > 1:
        for t in list(images):
            images[t ^ bit] = layout.along_row(images[t], bit)
            texts[t ^ bit] = layout.along_column(texts[t], bit)
        bit //= 2
    sources = [t for t in images if t]
    images[1] = layout.along_row(image_feats, 1)
    texts[1] = layout.along_column(text_feats, 1)
    for t in sources:
        images[t ^ 1] = layout.along_row(images[t], 1)
        texts[t ^ 1] = layout.along_column(texts[t], 1)
    images[0], texts[0], texts[1] = lax.optimization_barrier((image_feats, text_feats, texts[1]))
    for t in range(last):
        swap(t)
        project_next(t)
    images[last], texts[last], projected = lax.optimization_barrier(
        (images[last], texts[last], projected)
    )
    swap(last)
    first_width = width - 256
    results = block_grads(
        layout,
        first_width,
        scalars,
        image_proj,
        text_proj,
        [images[last], texts[last], *swapped[last]],
        [projected[t] for t in range(last)],
    )
    firsts, lates, stats = list(results[:side]), list(results[side : 2 * side]), results[-1]

    firsts[1:] = [layout.along_column(firsts[t], t) for t in range(1, side)]
    lates[1:] = [layout.along_row(lates[t], t) for t in range(1, side)]
    *firsts, stats = first_pieces(layout, firsts[0], stats, firsts[1:])

    firsts[1:] = [layout.along_row(firsts[t], t) for t in range(1, side)]
    lates, firsts[1] = lax.optimization_barrier((lates, firsts[1]))
    lates = list(late_pieces(layout, lates[0], lates[1:]))
    lates[1:] = [layout.along_column(lates[t], t) for t in range(1, side)]
    last_rows = 2 * out_rows
    first_sum = tree_sum([x[:last_rows].astype(F32) for x in firsts])
    late_sum = tree_sum([x.astype(F32) for x in lates])
    total = jnp.concatenate([first_sum, late_sum], axis=1)
    parts = [x[-8:-5, :384].astype(F32) for x in firsts[1:]]
    stat_total = tree_sum([stats[0]] + [x[0] + x[1] + x[2] for x in parts])

    upper, lower = total[:out_rows], total[out_rows:]
    keep, give = jnp.where(is_image, upper, lower), jnp.where(is_image, lower, upper)
    got = layout.sibling(give)
    image_proj_grad = jnp.where(is_image, keep, got)
    text_proj_grad = jnp.where(is_image, got, keep)
    stat_total = stat_total + layout.sibling(stat_total)
    totals = jnp.sum(stat_total.reshape(3, 128), axis=1) * (0.5 / batch_total)
    return totals[0:1], image_proj_grad, text_proj_grad, totals[1:2], totals[2:3]


def solution(mesh):
    layout = Layout(mesh.shape["dp"], mesh.shape["mp"])
    return jax.shard_map(
        functools.partial(per_device, layout),
        mesh=mesh,
        in_specs=(P(AXES, None), P(AXES, None), P(), P(), P(), P()),
        out_specs=(P(), P(AXES, None), P(AXES, None), P(), P()),
        check_vma=False,
    )
```

```python
import functools
import math

import jax
import jax.numpy as jnp
from jax import lax
from jax.experimental import pallas as pl
from jax.experimental.pallas import tpu as pltpu
from jax.sharding import PartitionSpec as P

F32 = jnp.float32
BF16 = jnp.bfloat16
AXES = ("dp", "mp")


class Layout:
    def __init__(self, dp_size, mp_size):
        self.dp, self.mp = dp_size, mp_size
        self.units = dp_size * mp_size // 2
        self.side = math.isqrt(self.units)
        if self.side * self.side != self.units or self.side % mp_size or self.side & (self.side - 1):
            raise ValueError("unsupported mesh")

    def device(self, unit, core):
        return (2 * (unit // self.mp) + core) * self.mp + unit % self.mp

    def send(self, value, step):
        s = self.side
        pairs = []
        for unit in range(self.units):
            for core in range(2):
                row, column, other = step(*divmod(unit, s), core)
                pairs.append((self.device(unit, core), self.device(row * s + column, other)))
        return lax.ppermute(value, AXES, pairs)

    def along_column(self, value, t):
        return self.send(value, lambda r, c, core: (r ^ t, c, core))

    def along_row(self, value, t):
        return self.send(value, lambda r, c, core: (r, c ^ t, core))

    def sibling(self, value):
        return self.send(value, lambda r, c, core: (r, c, 1 - core))


def tree_sum(values):
    values = list(values)
    while len(values) > 1:
        values = [a + b for a, b in zip(values[::2], values[1::2])]
    return values[0]


def this_core():
    return lax.rem(lax.axis_index("dp"), 2)


def load_projections(image_proj, text_proj, projs, sems):
    core = this_core()
    own = pltpu.make_async_copy(image_proj, projs.at[core], sems.at[0])
    other = pltpu.make_async_copy(text_proj, projs.at[1 - core], sems.at[1])
    own.start()
    other.start()
    return [own, other]


def load_chunk(shards, feats, sems):
    core = this_core()
    rows = shards[0].shape[0]
    copies = []
    for i, shard in enumerate(shards):
        place = pl.ds((core if i < 2 else 1 - core) * rows, rows)
        side = core if i % 2 == 0 else 1 - core
        copies.append(pltpu.make_async_copy(shard, feats.at[side, place], sems.at[i]))
        copies[-1].start()
    return copies


def project(rows, projection):
    raw = jnp.dot(rows, projection, preferred_element_type=F32)
    inverse = lax.rsqrt(jnp.sum(raw * raw, axis=-1, keepdims=True) + 1e-06)
    return raw * inverse, inverse


def project_kernel(image_proj, text_proj, *refs):
    shards, (own_chunk, own_unit, own_inverse, other_half, feats, projs, sems) = refs[:4], refs[4:]
    copies = load_chunk(shards, feats, sems.at[pl.ds(2, 4)])
    copies += load_projections(image_proj, text_proj, projs, sems.at[pl.ds(0, 2)])
    for copy in copies:
        copy.wait()
    unit, _ = project(feats[1], projs[1])
    other_half[...] = unit.astype(BF16)
    unit, inverse = project(feats[0], projs[0])
    own_unit[...] = unit
    own_inverse[...] = jnp.broadcast_to(inverse, own_inverse.shape)
    own_chunk[...] = feats[0]


def project_chunk(image_proj, text_proj, shards, from_arguments):
    rows, width = shards[0].shape
    rows = 2 * rows
    anywhere = pl.BlockSpec(memory_space=pl.ANY)
    hbm = pl.BlockSpec(memory_space=pltpu.HBM)
    vmem = pl.BlockSpec(memory_space=pltpu.VMEM)
    return pl.pallas_call(
        project_kernel,
        out_shape=[
            jax.ShapeDtypeStruct((rows, width), BF16),
            jax.ShapeDtypeStruct((rows, width), F32),
            jax.ShapeDtypeStruct((rows, 128), F32),
            jax.ShapeDtypeStruct((rows, width), BF16),
        ],
        in_specs=[hbm] * 2 + [hbm if from_arguments else anywhere] * 2 + [anywhere] * 2,
        out_specs=[vmem] * 4,
        scratch_shapes=[
            pltpu.VMEM((2, rows, width), BF16),
            pltpu.VMEM((2, width, width), BF16),
            pltpu.SemaphoreType.DMA((6,)),
        ],
        compiler_params=pltpu.CompilerParams(
            vmem_limit_bytes=4 * width * width + 24 * rows * width + 4 * 1024 * 1024
        ),
        cost_estimate=pl.CostEstimate(
            flops=4 * rows * width * width,
            bytes_accessed=4 * width * width + 12 * rows * width,
            transcendentals=2 * rows,
        ),
        name="project",
    )(image_proj, text_proj, *shards)


def pair_terms(cosine, scale, bias, masked):
    logits = scale * cosine + bias
    small = jnp.exp(-jnp.abs(logits))
    inverse_sum = 1.0 / (1.0 + small)
    large_side = logits >= 0.0
    pair_grads = jnp.where(large_side, inverse_sum, small * inverse_sum)
    tops = jnp.maximum(logits, 0.0)
    if masked:
        equal = lax.broadcasted_iota(jnp.int32, cosine.shape, 0) == lax.broadcasted_iota(
            jnp.int32, cosine.shape, 1
        )
        lower = jnp.where(large_side, small * inverse_sum, inverse_sum)
        pair_grads = jnp.where(equal, -lower, pair_grads)
        tops = jnp.where(equal, jnp.maximum(-logits, 0.0), tops)
    return tops + jnp.log1p(small), pair_grads


def lane_sums(values):
    total = jnp.sum(values, axis=0, keepdims=True)
    return sum(total[:, j : j + 128] for j in range(0, total.shape[1], 128))


def block_kernel(side, mp_size, first_width, scalars, image_proj, text_proj, *refs):
    last_shards, refs = refs[:4], refs[4:]
    own_chunks, refs = refs[: side - 1], refs[side - 1 :]
    own_units, refs = refs[: side - 1], refs[side - 1 :]
    own_inverses, refs = refs[: side - 1], refs[side - 1 :]
    other_halves, refs = refs[: side - 1], refs[side - 1 :]
    firsts, refs = refs[:side], refs[side:]
    own_late, late_message, refs = refs[0], refs[1], refs[2:]
    stats, projs, last, feats, units, inverses, other_half, dy, grad, piece, sems = refs
    rows, width = dy.shape
    chunk_rows = rows // side
    rest = rows - chunk_rows
    dp_index, mp_index = lax.axis_index("dp"), lax.axis_index("mp")
    unit_index = dp_index // 2 * mp_size + mp_index
    unit_row, unit_column = unit_index // side, lax.rem(unit_index, side)
    scale, bias = scalars[0], scalars[1]

    count = 6

    def start(source, target):
        nonlocal count
        copy = pltpu.make_async_copy(source, target, sems.at[count])
        copy.start()
        count += 1
        return copy

    def places(i):
        return pl.ds(i * chunk_rows, chunk_rows)

    first_copies = load_chunk(last_shards, last, sems.at[pl.ds(2, 4)])
    first_copies += load_projections(image_proj, text_proj, projs, sems.at[pl.ds(0, 2)])
    other_copies = [start(other_halves[i], other_half.at[places(i)]) for i in range(side - 1)]
    unit_copies = [start(own_units[i], units.at[places(i)]) for i in range(side - 1)]
    unit_copies += [start(own_inverses[i], inverses.at[places(i)]) for i in range(side - 1)]
    feat_copies = [start(own_chunks[i], feats.at[places(i)]) for i in range(side - 1)]

    for copy in first_copies:
        copy.wait()
    unit, _ = project(last[1], projs[1])
    other_half[rest:, :] = unit.astype(BF16)
    unit, inverse = project(last[0], projs[0])
    units[rest:, :] = unit
    inverses[rest:, :] = jnp.broadcast_to(inverse, (chunk_rows, 128))
    feats[rest:, :] = last[0]
    for copy in other_copies + unit_copies:
        copy.wait()

    def tile(place, with_partners):
        unit = units[place, :]
        cosine = lax.dot_general(
            unit.astype(BF16), other_half[...], (((1,), (1,)), ((), ())), preferred_element_type=F32
        )
        if with_partners:
            terms = [
                pair_terms(cosine[:, :chunk_rows], scale, bias, True),
                pair_terms(cosine[:, chunk_rows:], scale, bias, False),
            ]
            losses, pair_grads = [jnp.concatenate(x, axis=1) for x in zip(*terms)]
        else:
            losses, pair_grads = pair_terms(cosine, scale, bias, False)
        half_grads = pair_grads.astype(BF16)
        sums = jnp.concatenate(
            [lane_sums(losses), lane_sums(pair_grads * cosine) * scale, lane_sums(pair_grads)], axis=1
        )
        stats[0:1, :] = sums if with_partners else stats[0:1, :] + sums
        inner = jnp.sum(half_grads.astype(F32) * cosine, axis=-1, keepdims=True)
        grads = jnp.dot(half_grads, other_half[...], preferred_element_type=F32)
        dy[place, :] = ((grads - unit * inner) * (scale * inverses[place, 0:1])).astype(BF16)

    tile(pl.ds(0, chunk_rows), True)

    @pl.loop(1, side)
    def _(i):
        tile(pl.ds(pl.multiple_of(i * chunk_rows, chunk_rows), chunk_rows), False)

    for copy in feat_copies:
        copy.wait()
    for j in range(0, width, 128):
        grad[j : j + 128, :] = lax.dot_general(
            feats[:, j : j + 128], dy[...], (((0,), (0,)), ((), ())), preferred_element_type=F32
        )

    sums = stats[0:1, :]
    stats[...] = jnp.broadcast_to(sums, stats.shape)
    chunk = width // side
    for t in range(side):
        first = pl.multiple_of(jnp.bitwise_xor(unit_row, t) * chunk, chunk)
        firsts[t][:chunk, :] = grad[pl.ds(first, chunk), :first_width].astype(firsts[t].dtype)
        if t:
            firsts[t][chunk:, :] = stat_rows(sums, first_width).astype(BF16)
    out_rows = chunk // (2 * side)
    for column in range(side):
        for i in range(side):
            for core in range(2):
                source = i * chunk + shard_of(column, core, mp_size) * out_rows
                target = (2 * i + core) * out_rows
                piece[target : target + out_rows, :] = grad[source : source + out_rows, first_width:]
        half = side // 2 * chunk
        for t in range(side):
            target = own_late if t < side // 2 else late_message
            place = pl.ds(t * chunk % half, chunk)
            store_for(column, unit_column, piece, {t: target.at[place, :]})


def shard_of(column, core, mp_size):
    return column // mp_size * 2 * mp_size + core * mp_size + column % mp_size


def store_for(index, own_index, piece, outs):
    for t, out in outs.items():

        @pl.when(jnp.bitwise_xor(own_index, t) == index)
        def _():
            out[...] = piece[...].astype(out.dtype)


def stat_rows(sums, width):
    part0 = sums.astype(BF16).astype(F32)
    part1 = (sums - part0).astype(BF16).astype(F32)
    part2 = sums - part0 - part1
    line = lax.broadcasted_iota(jnp.int32, (8, sums.shape[1]), 0)
    parts = jnp.where(line == 0, part0, jnp.where(line == 1, part1, jnp.where(line == 2, part2, 0.0)))
    if width > sums.shape[1]:
        parts = jnp.concatenate([parts, jnp.zeros((8, width - sums.shape[1]), F32)], axis=1)
    return parts


def block_grads(layout, first_width, scalars, image_proj, text_proj, last_shards, projected):
    side = layout.side
    chunk_rows, width = projected[0][0].shape
    rows = side * chunk_rows
    chunk = width // side
    anywhere = pl.BlockSpec(memory_space=pl.ANY)
    vmem = pl.BlockSpec(memory_space=pltpu.VMEM)
    late_width = width - first_width
    operands = [image_proj, text_proj, *last_shards]
    operands += [x for column in zip(*projected) for x in column]
    needed = 4 * width * width + 12 * rows * width + 4 * chunk_rows * width
    needed += 4 * width * (width + late_width) + 24 * chunk_rows * rows + 7 * 1024 * 1024
    return pl.pallas_call(
        functools.partial(block_kernel, side, layout.mp, first_width),
        out_shape=[jax.ShapeDtypeStruct((chunk, first_width), F32)]
        + [jax.ShapeDtypeStruct((chunk + 8, first_width), BF16)] * (side - 1)
        + [jax.ShapeDtypeStruct((width // 2, late_width), F32)]
        + [jax.ShapeDtypeStruct((width // 2, late_width), BF16)]
        + [jax.ShapeDtypeStruct((8, 384), F32)],
        in_specs=[pl.BlockSpec(memory_space=pltpu.SMEM)]
        + [pl.BlockSpec(memory_space=pltpu.HBM)] * 2
        + [anywhere] * (len(operands) - 2),
        out_specs=[vmem] * (side + 3),
        scratch_shapes=[
            pltpu.VMEM((2, width, width), BF16),
            pltpu.VMEM((2, chunk_rows, width), BF16),
            pltpu.VMEM((rows, width), BF16),
            pltpu.VMEM((rows, width), F32),
            pltpu.VMEM((rows, 128), F32),
            pltpu.VMEM((rows, width), BF16),
            pltpu.VMEM((rows, width), BF16),
            pltpu.VMEM((width, width), F32),
            pltpu.VMEM((chunk, late_width), F32),
            pltpu.SemaphoreType.DMA((len(operands),)),
        ],
        compiler_params=pltpu.CompilerParams(vmem_limit_bytes=min(needed, 60 * 1024 * 1024)),
        cost_estimate=pl.CostEstimate(
            flops=2 * rows * width * (2 * rows + width) + 4 * chunk_rows * width * width,
            bytes_accessed=12 * rows * width + 4 * width * width,
            transcendentals=3 * rows * rows,
        ),
        name="block",
    )(scalars, *operands)


def arrived_sum(own, arrived, rows):
    return tree_sum([own[:rows, :]] + [x[:rows, :].astype(F32) for x in arrived])


def first_kernel(side, mp_size, own, own_stats, *refs):
    arrived, outs = refs[: side - 1], refs[side - 1 : 2 * side - 1]
    stats, total, piece = refs[2 * side - 1 :]
    chunk, width = own.shape
    out_rows = chunk // (2 * side)
    total[...] = arrived_sum(own, arrived, chunk)
    parts = [x[chunk:, :384].astype(F32) for x in arrived]
    sums = tree_sum([own_stats[0:1, :]] + [x[0:1] + x[1:2] + x[2:3] for x in parts])
    stats[...] = jnp.broadcast_to(sums, stats.shape)
    dp_index, mp_index = lax.axis_index("dp"), lax.axis_index("mp")
    unit_column = lax.rem(dp_index // 2 * mp_size + mp_index, side)
    piece[2 * out_rows :, :] = jnp.zeros((piece.shape[0] - 2 * out_rows, width), F32)
    piece[piece.shape[0] - 8 :, :] = stat_rows(sums, width)
    for column in range(side):
        for core in range(2):
            source = shard_of(column, core, mp_size) * out_rows
            piece[core * out_rows : (core + 1) * out_rows, :] = total[source : source + out_rows, :]
        store_for(column, unit_column, piece, dict(enumerate(outs)))


def first_pieces(layout, own, own_stats, arrived):
    side = layout.side
    chunk, width = own.shape
    rows = (2 * (chunk // (2 * side)) + 7) // 8 * 8 + 8
    vmem = pl.BlockSpec(memory_space=pltpu.VMEM)
    return pl.pallas_call(
        functools.partial(first_kernel, side, layout.mp),
        out_shape=[jax.ShapeDtypeStruct((rows, width), F32)]
        + [jax.ShapeDtypeStruct((rows, width), BF16)] * (side - 1)
        + [jax.ShapeDtypeStruct((8, 384), F32)],
        in_specs=[vmem] * (side + 1),
        out_specs=[vmem] * (side + 1),
        scratch_shapes=[pltpu.VMEM((chunk, width), F32), pltpu.VMEM((rows, width), F32)],
        compiler_params=pltpu.CompilerParams(vmem_limit_bytes=12 * 1024 * 1024),
        name="first",
    )(own, own_stats, *arrived)


def halve_kernel(own, arrived, keep, message):
    half = keep.shape[0]
    keep[...] = own[:half, :] + arrived[:half, :].astype(F32)
    message[...] = (own[half:, :] + arrived[half:, :].astype(F32)).astype(BF16)


def halve(own, arrived):
    rows, width = own.shape
    vmem = pl.BlockSpec(memory_space=pltpu.VMEM)
    return pl.pallas_call(
        halve_kernel,
        out_shape=[
            jax.ShapeDtypeStruct((rows // 2, width), F32),
            jax.ShapeDtypeStruct((rows // 2, width), BF16),
        ],
        in_specs=[vmem] * 2,
        out_specs=[vmem] * 2,
        compiler_params=pltpu.CompilerParams(vmem_limit_bytes=12 * 1024 * 1024),
        name="halve",
    )(own, arrived)


def late_kernel(side, mp_size, own, *refs):
    arrived, outs, total = refs[:1], refs[1:-1], refs[-1]
    chunk = own.shape[0]
    total[...] = arrived_sum(own, arrived, chunk)
    dp_index, mp_index = lax.axis_index("dp"), lax.axis_index("mp")
    unit_row = (dp_index // 2 * mp_size + mp_index) // side
    rows = chunk // side
    for row in range(side):
        piece = total.at[row * rows : (row + 1) * rows, :]
        store_for(row, unit_row, piece, dict(enumerate(outs)))


def late_pieces(layout, own, arrived):
    side = layout.side
    chunk, width = own.shape
    rows = chunk // side
    vmem = pl.BlockSpec(memory_space=pltpu.VMEM)
    return pl.pallas_call(
        functools.partial(late_kernel, side, layout.mp),
        out_shape=[jax.ShapeDtypeStruct((rows, width), F32)]
        + [jax.ShapeDtypeStruct((rows, width), BF16)] * (side - 1),
        in_specs=[vmem] * 2,
        out_specs=[vmem] * side,
        scratch_shapes=[pltpu.VMEM((chunk, width), F32)],
        compiler_params=pltpu.CompilerParams(vmem_limit_bytes=12 * 1024 * 1024),
        name="late",
    )(own, arrived)


def per_device(layout, image_feats, text_feats, image_proj, text_proj, log_scale, logit_bias):
    side = layout.side
    own_rows, width = image_feats.shape
    devices = layout.dp * layout.mp
    out_rows = width // devices
    batch_total = own_rows * devices
    is_image = lax.axis_index("dp") % 2 == 0

    scalars = jnp.concatenate([jnp.exp(log_scale), logit_bias])

    images, texts, swapped, projected = {0: image_feats}, {0: text_feats}, {}, {}

    def swap(t):
        swapped[t] = layout.sibling(images[t]), layout.sibling(texts[t])

    def project_next(t):
        shards = [images[t], texts[t], *swapped[t]]
        projected[t] = project_chunk(image_proj, text_proj, shards, t == 0)

    last = side - 1
    bit = side // 2
    while bit > 1:
        for t in list(images):
            images[t ^ bit] = layout.along_row(images[t], bit)
            texts[t ^ bit] = layout.along_column(texts[t], bit)
        bit //= 2
    sources = [t for t in images if t]
    images[1] = layout.along_row(image_feats, 1)
    texts[1] = layout.along_column(text_feats, 1)
    swap(0)
    project_next(0)
    images, texts, projected = lax.optimization_barrier((images, texts, projected))
    for t in sources:
        images[t ^ 1] = layout.along_row(images[t], 1)
        texts[t ^ 1] = layout.along_column(texts[t], 1)
    for t in range(1, last):
        swap(t)
        project_next(t)
    images[last], texts[last], projected = lax.optimization_barrier(
        (images[last], texts[last], projected)
    )
    swap(last)
    first_width = width - width // 3
    results = block_grads(
        layout,
        first_width,
        scalars,
        image_proj,
        text_proj,
        [images[last], texts[last], *swapped[last]],
        [projected[t] for t in range(last)],
    )
    firsts, (late, message, stats) = list(results[:side]), results[side:]

    firsts[1:] = [layout.along_column(firsts[t], t) for t in range(1, side)]
    bit = side // 2
    arrived = layout.along_row(message, bit)
    while bit > 1:
        late, message = halve(late, arrived)
        bit //= 2
        arrived = layout.along_row(message, bit)
    *firsts, stats = first_pieces(layout, firsts[0], stats, firsts[1:])

    firsts[1:] = [layout.along_row(firsts[t], t) for t in range(1, side)]
    lates = list(late_pieces(layout, late, arrived))
    lates[1:] = [layout.along_column(lates[t], t) for t in range(1, side)]
    firsts, lates = lax.optimization_barrier((firsts, lates))
    last_rows = 2 * out_rows
    first_sum = tree_sum([x[:last_rows].astype(F32) for x in firsts])
    late_sum = tree_sum([x.astype(F32) for x in lates])
    total = jnp.concatenate([first_sum, late_sum], axis=1)
    parts = [x[-8:-5, :384].astype(F32) for x in firsts[1:]]
    stat_total = tree_sum([stats[0]] + [x[0] + x[1] + x[2] for x in parts])

    upper, lower = total[:out_rows], total[out_rows:]
    keep, give = jnp.where(is_image, upper, lower), jnp.where(is_image, lower, upper)
    got = layout.sibling(give)
    image_proj_grad = jnp.where(is_image, keep, got)
    text_proj_grad = jnp.where(is_image, got, keep)
    stat_total = stat_total + layout.sibling(stat_total)
    totals = jnp.sum(stat_total.reshape(3, 128), axis=1) * (0.5 / batch_total)
    return totals[0:1], image_proj_grad, text_proj_grad, totals[1:2], totals[2:3]


def solution(mesh):
    layout = Layout(mesh.shape["dp"], mesh.shape["mp"])
    return jax.shard_map(
        functools.partial(per_device, layout),
        mesh=mesh,
        in_specs=(P(AXES, None), P(AXES, None), P(), P(), P(), P()),
        out_specs=(P(), P(AXES, None), P(AXES, None), P(), P()),
        check_vma=False,
    )
```

```python
import functools
import math

import jax
import jax.numpy as jnp
from jax import lax
from jax.experimental import pallas as pl
from jax.experimental.pallas import tpu as pltpu
from jax.sharding import PartitionSpec as P

F32 = jnp.float32
BF16 = jnp.bfloat16
AXES = ("dp", "mp")


class Layout:
    def __init__(self, dp_size, mp_size):
        self.dp, self.mp = dp_size, mp_size
        self.units = dp_size * mp_size // 2
        self.side = math.isqrt(self.units)
        if self.side * self.side != self.units or self.side % mp_size or self.side & (self.side - 1):
            raise ValueError("unsupported mesh")

    def device(self, unit, core):
        return (2 * (unit // self.mp) + core) * self.mp + unit % self.mp

    def send(self, value, step):
        s = self.side
        pairs = []
        for unit in range(self.units):
            for core in range(2):
                row, column, other = step(*divmod(unit, s), core)
                pairs.append((self.device(unit, core), self.device(row * s + column, other)))
        return lax.ppermute(value, AXES, pairs)

    def along_column(self, value, t):
        return self.send(value, lambda r, c, core: (r ^ t, c, core))

    def along_row(self, value, t):
        return self.send(value, lambda r, c, core: (r, c ^ t, core))

    def sibling(self, value):
        return self.send(value, lambda r, c, core: (r, c, 1 - core))


def tree_sum(values):
    values = list(values)
    while len(values) > 1:
        values = [a + b for a, b in zip(values[::2], values[1::2])]
    return values[0]


def this_core():
    return lax.rem(lax.axis_index("dp"), 2)


def load_projections(image_proj, text_proj, projs, sems):
    core = this_core()
    own = pltpu.make_async_copy(image_proj, projs.at[core], sems.at[0])
    other = pltpu.make_async_copy(text_proj, projs.at[1 - core], sems.at[1])
    own.start()
    other.start()
    return [own, other]


def load_chunk(shards, feats, sems):
    core = this_core()
    rows = shards[0].shape[0]
    copies = []
    for i, shard in enumerate(shards):
        place = pl.ds((core if i < 2 else 1 - core) * rows, rows)
        side = core if i % 2 == 0 else 1 - core
        copies.append(pltpu.make_async_copy(shard, feats.at[side, place], sems.at[i]))
        copies[-1].start()
    return copies


def project(rows, projection):
    raw = jnp.dot(rows, projection, preferred_element_type=F32)
    inverse = lax.rsqrt(jnp.sum(raw * raw, axis=-1, keepdims=True) + 1e-06)
    return raw * inverse, inverse


def project_kernel(image_proj, text_proj, *refs):
    shards, (own_chunk, own_unit, own_inverse, other_half, feats, projs, sems) = refs[:4], refs[4:]
    copies = load_chunk(shards, feats, sems.at[pl.ds(2, 4)])
    copies += load_projections(image_proj, text_proj, projs, sems.at[pl.ds(0, 2)])
    for copy in copies:
        copy.wait()
    unit, _ = project(feats[1], projs[1])
    other_half[...] = unit.astype(BF16)
    unit, inverse = project(feats[0], projs[0])
    own_unit[...] = unit
    own_inverse[...] = jnp.broadcast_to(inverse, own_inverse.shape)
    own_chunk[...] = feats[0]


def project_chunk(image_proj, text_proj, shards, from_arguments):
    rows, width = shards[0].shape
    rows = 2 * rows
    anywhere = pl.BlockSpec(memory_space=pl.ANY)
    hbm = pl.BlockSpec(memory_space=pltpu.HBM)
    vmem = pl.BlockSpec(memory_space=pltpu.VMEM)
    return pl.pallas_call(
        project_kernel,
        out_shape=[
            jax.ShapeDtypeStruct((rows, width), BF16),
            jax.ShapeDtypeStruct((rows, width), F32),
            jax.ShapeDtypeStruct((rows, 128), F32),
            jax.ShapeDtypeStruct((rows, width), BF16),
        ],
        in_specs=[hbm] * 2 + [hbm if from_arguments else anywhere] * 2 + [anywhere] * 2,
        out_specs=[vmem] * 4,
        scratch_shapes=[
            pltpu.VMEM((2, rows, width), BF16),
            pltpu.VMEM((2, width, width), BF16),
            pltpu.SemaphoreType.DMA((6,)),
        ],
        compiler_params=pltpu.CompilerParams(
            vmem_limit_bytes=4 * width * width + 24 * rows * width + 4 * 1024 * 1024
        ),
        cost_estimate=pl.CostEstimate(
            flops=4 * rows * width * width,
            bytes_accessed=4 * width * width + 12 * rows * width,
            transcendentals=2 * rows,
        ),
        name="project",
    )(image_proj, text_proj, *shards)


def pair_terms(cosine, scale, bias, masked):
    logits = scale * cosine + bias
    raised = jnp.exp(logits)
    total = 1.0 + raised
    inverse = 1.0 / total
    losses = jnp.log(total) + (raised - (total - 1.0)) * inverse
    pair_grads = raised * inverse
    if masked:
        equal = lax.broadcasted_iota(jnp.int32, cosine.shape, 0) == lax.broadcasted_iota(
            jnp.int32, cosine.shape, 1
        )
        losses = jnp.where(equal, jnp.log1p(jnp.exp(-logits)), losses)
        pair_grads = jnp.where(equal, -inverse, pair_grads)
    return losses, pair_grads


def lane_sums(values):
    total = jnp.sum(values, axis=0, keepdims=True)
    return sum(total[:, j : j + 128] for j in range(0, total.shape[1], 128))


def block_kernel(side, mp_size, groups, scalars, image_proj, text_proj, *refs):
    last_shards, refs = refs[:4], refs[4:]
    own_chunks, refs = refs[: side - 1], refs[side - 1 :]
    own_units, refs = refs[: side - 1], refs[side - 1 :]
    own_inverses, refs = refs[: side - 1], refs[side - 1 :]
    other_halves, refs = refs[: side - 1], refs[side - 1 :]
    firsts, refs = refs[: side * len(groups)], refs[side * len(groups) :]
    own_late, late_message, refs = refs[0], refs[1], refs[2:]
    stats, projs, last, feats, units, inverses, other_half, dy, grad, piece, sems = refs
    rows, width = dy.shape
    chunk_rows = rows // side
    rest = rows - chunk_rows
    dp_index, mp_index = lax.axis_index("dp"), lax.axis_index("mp")
    unit_index = dp_index // 2 * mp_size + mp_index
    unit_row, unit_column = unit_index // side, lax.rem(unit_index, side)
    scale, bias = scalars[0], scalars[1]

    count = 6

    def start(source, target):
        nonlocal count
        copy = pltpu.make_async_copy(source, target, sems.at[count])
        copy.start()
        count += 1
        return copy

    def places(i):
        return pl.ds(i * chunk_rows, chunk_rows)

    first_copies = load_chunk(last_shards, last, sems.at[pl.ds(2, 4)])
    first_copies += load_projections(image_proj, text_proj, projs, sems.at[pl.ds(0, 2)])
    other_copies = [start(other_halves[i], other_half.at[places(i)]) for i in range(side - 1)]
    unit_copies = [start(own_units[i], units.at[places(i)]) for i in range(side - 1)]
    unit_copies += [start(own_inverses[i], inverses.at[places(i)]) for i in range(side - 1)]
    feat_copies = [start(own_chunks[i], feats.at[places(i)]) for i in range(side - 1)]

    for copy in first_copies:
        copy.wait()
    unit, _ = project(last[1], projs[1])
    other_half[rest:, :] = unit.astype(BF16)
    unit, inverse = project(last[0], projs[0])
    units[rest:, :] = unit
    inverses[rest:, :] = jnp.broadcast_to(inverse, (chunk_rows, 128))
    feats[rest:, :] = last[0]
    for copy in other_copies + unit_copies:
        copy.wait()

    def cosines(i):
        half = units[i * chunk_rows : (i + 1) * chunk_rows, :].astype(BF16)
        return lax.dot_general(
            half, other_half[...], (((1,), (1,)), ((), ())), preferred_element_type=F32
        )

    total = None
    cosine = cosines(0)
    for i in range(side):
        following = cosines(i + 1) if i + 1 < side else None
        if i == 0:
            terms = [
                pair_terms(cosine[:, :chunk_rows], scale, bias, True),
                pair_terms(cosine[:, chunk_rows:], scale, bias, False),
            ]
            losses, pair_grads = [jnp.concatenate(x, axis=1) for x in zip(*terms)]
        else:
            losses, pair_grads = pair_terms(cosine, scale, bias, False)
        half_grads = pair_grads.astype(BF16)
        sums = [lane_sums(losses), lane_sums(pair_grads * cosine) * scale, lane_sums(pair_grads)]
        sums = jnp.concatenate(sums, axis=1)
        total = sums if total is None else total + sums
        inner = jnp.sum(half_grads.astype(F32) * cosine, axis=-1, keepdims=True)
        grads = jnp.dot(half_grads, other_half[...], preferred_element_type=F32)
        place = slice(i * chunk_rows, (i + 1) * chunk_rows)
        grads = (grads - units[place, :] * inner) * (scale * inverses[place, 0:1])
        dy[place, :] = grads.astype(BF16)
        cosine = following
    stats[0:1, :] = total

    for copy in feat_copies:
        copy.wait()
    for j in range(0, width, 128):
        grad[j : j + 128, :] = lax.dot_general(
            feats[:, j : j + 128], dy[...], (((0,), (0,)), ((), ())), preferred_element_type=F32
        )

    sums = stats[0:1, :]
    stats[...] = jnp.broadcast_to(sums, stats.shape)
    chunk = width // side
    for g, (begin, end) in enumerate(groups):
        for t in range(side):
            out = firsts[side * g + t]
            first = pl.multiple_of(jnp.bitwise_xor(unit_row, t) * chunk, chunk)
            out[:chunk, :] = grad[pl.ds(first, chunk), begin:end].astype(out.dtype)
            if t and g == 0:
                out[chunk:, :] = stat_rows(sums, end - begin).astype(BF16)
    first_width = groups[-1][1]
    out_rows = chunk // (2 * side)
    for column in range(side):
        for i in range(side):
            for core in range(2):
                source = i * chunk + shard_of(column, core, mp_size) * out_rows
                target = (2 * i + core) * out_rows
                piece[target : target + out_rows, :] = grad[source : source + out_rows, first_width:]
        half = side // 2 * chunk
        for t in range(side):
            target = own_late if t < side // 2 else late_message
            place = pl.ds(t * chunk % half, chunk)
            store_for(column, unit_column, piece, {t: target.at[place, :]})


def shard_of(column, core, mp_size):
    return column // mp_size * 2 * mp_size + core * mp_size + column % mp_size


def store_for(index, own_index, piece, outs):
    for t, out in outs.items():

        @pl.when(jnp.bitwise_xor(own_index, t) == index)
        def _():
            out[...] = piece[...].astype(out.dtype)


def stat_rows(sums, width):
    part0 = sums.astype(BF16).astype(F32)
    part1 = (sums - part0).astype(BF16).astype(F32)
    part2 = sums - part0 - part1
    line = lax.broadcasted_iota(jnp.int32, (8, sums.shape[1]), 0)
    parts = jnp.where(line == 0, part0, jnp.where(line == 1, part1, jnp.where(line == 2, part2, 0.0)))
    if width > sums.shape[1]:
        parts = jnp.concatenate([parts, jnp.zeros((8, width - sums.shape[1]), F32)], axis=1)
    return parts


def block_grads(layout, groups, scalars, image_proj, text_proj, last_shards, projected):
    side = layout.side
    chunk_rows, width = projected[0][0].shape
    rows = side * chunk_rows
    chunk = width // side
    anywhere = pl.BlockSpec(memory_space=pl.ANY)
    vmem = pl.BlockSpec(memory_space=pltpu.VMEM)
    first_width = groups[-1][1]
    late_width = width - first_width
    operands = [image_proj, text_proj, *last_shards]
    operands += [x for column in zip(*projected) for x in column]
    out_shape = []
    for begin, end in groups:
        out_shape.append(jax.ShapeDtypeStruct((chunk, end - begin), F32))
        message = jax.ShapeDtypeStruct((chunk if begin else chunk + 8, end - begin), BF16)
        out_shape += [message] * (side - 1)
    needed = 4 * width * width + 12 * rows * width + 4 * chunk_rows * width
    needed += 4 * width * (width + late_width) + 24 * chunk_rows * rows + 7 * 1024 * 1024
    return pl.pallas_call(
        functools.partial(block_kernel, side, layout.mp, groups),
        out_shape=out_shape
        + [jax.ShapeDtypeStruct((width // 2, late_width), F32)]
        + [jax.ShapeDtypeStruct((width // 2, late_width), BF16)]
        + [jax.ShapeDtypeStruct((8, 384), F32)],
        in_specs=[pl.BlockSpec(memory_space=pltpu.SMEM)]
        + [pl.BlockSpec(memory_space=pltpu.HBM)] * 2
        + [anywhere] * (len(operands) - 2),
        out_specs=[vmem] * (len(out_shape) + 3),
        scratch_shapes=[
            pltpu.VMEM((2, width, width), BF16),
            pltpu.VMEM((2, chunk_rows, width), BF16),
            pltpu.VMEM((rows, width), BF16),
            pltpu.VMEM((rows, width), F32),
            pltpu.VMEM((rows, 128), F32),
            pltpu.VMEM((rows, width), BF16),
            pltpu.VMEM((rows, width), BF16),
            pltpu.VMEM((width, width), F32),
            pltpu.VMEM((chunk, late_width), F32),
            pltpu.SemaphoreType.DMA((len(operands),)),
        ],
        compiler_params=pltpu.CompilerParams(vmem_limit_bytes=min(needed, 60 * 1024 * 1024)),
        cost_estimate=pl.CostEstimate(
            flops=2 * rows * width * (2 * rows + width) + 4 * chunk_rows * width * width,
            bytes_accessed=12 * rows * width + 4 * width * width,
            transcendentals=3 * rows * rows,
        ),
        name="block",
    )(scalars, *operands)


def arrived_sum(own, arrived, rows):
    return tree_sum([own[:rows, :]] + [x[:rows, :].astype(F32) for x in arrived])


def first_kernel(side, mp_size, has_stats, own, *refs):
    own_stats, refs = (refs[0], refs[1:]) if has_stats else (None, refs)
    arrived, outs, refs = refs[: side - 1], refs[side - 1 : 2 * side - 1], refs[2 * side - 1 :]
    total, piece = refs[-2:]
    chunk, width = own.shape
    out_rows = chunk // (2 * side)
    total[...] = arrived_sum(own, arrived, chunk)
    if piece.shape[0] > 2 * out_rows:
        piece[2 * out_rows :, :] = jnp.zeros((piece.shape[0] - 2 * out_rows, width), F32)
    if has_stats:
        parts = [x[chunk:, :384].astype(F32) for x in arrived]
        sums = tree_sum([own_stats[0:1, :]] + [x[0:1] + x[1:2] + x[2:3] for x in parts])
        refs[0][...] = jnp.broadcast_to(sums, refs[0].shape)
        piece[piece.shape[0] - 8 :, :] = stat_rows(sums, width)
    dp_index, mp_index = lax.axis_index("dp"), lax.axis_index("mp")
    unit_column = lax.rem(dp_index // 2 * mp_size + mp_index, side)
    for column in range(side):
        for core in range(2):
            source = shard_of(column, core, mp_size) * out_rows
            piece[core * out_rows : (core + 1) * out_rows, :] = total[source : source + out_rows, :]
        store_for(column, unit_column, piece, dict(enumerate(outs)))


def first_pieces(layout, own, own_stats, arrived):
    side = layout.side
    chunk, width = own.shape
    has_stats = own_stats is not None
    rows = (2 * (chunk // (2 * side)) + 7) // 8 * 8 + (8 if has_stats else 0)
    vmem = pl.BlockSpec(memory_space=pltpu.VMEM)
    out_shape = [jax.ShapeDtypeStruct((rows, width), F32)]
    out_shape += [jax.ShapeDtypeStruct((rows, width), BF16)] * (side - 1)
    operands = [own, *([own_stats] if has_stats else []), *arrived]
    if has_stats:
        out_shape.append(jax.ShapeDtypeStruct((8, 384), F32))
    return pl.pallas_call(
        functools.partial(first_kernel, side, layout.mp, has_stats),
        out_shape=out_shape,
        in_specs=[vmem] * len(operands),
        out_specs=[vmem] * len(out_shape),
        scratch_shapes=[pltpu.VMEM((chunk, width), F32), pltpu.VMEM((rows, width), F32)],
        compiler_params=pltpu.CompilerParams(vmem_limit_bytes=12 * 1024 * 1024),
        name="first",
    )(*operands)


def halve_kernel(own, arrived, keep, message):
    half = keep.shape[0]
    keep[...] = own[:half, :] + arrived[:half, :].astype(F32)
    message[...] = (own[half:, :] + arrived[half:, :].astype(F32)).astype(BF16)


def halve(own, arrived):
    rows, width = own.shape
    vmem = pl.BlockSpec(memory_space=pltpu.VMEM)
    return pl.pallas_call(
        halve_kernel,
        out_shape=[
            jax.ShapeDtypeStruct((rows // 2, width), F32),
            jax.ShapeDtypeStruct((rows // 2, width), BF16),
        ],
        in_specs=[vmem] * 2,
        out_specs=[vmem] * 2,
        compiler_params=pltpu.CompilerParams(vmem_limit_bytes=12 * 1024 * 1024),
        name="halve",
    )(own, arrived)


def late_kernel(side, mp_size, own, *refs):
    arrived, outs, total = refs[:1], refs[1:-1], refs[-1]
    chunk = own.shape[0]
    total[...] = arrived_sum(own, arrived, chunk)
    dp_index, mp_index = lax.axis_index("dp"), lax.axis_index("mp")
    unit_row = (dp_index // 2 * mp_size + mp_index) // side
    rows = chunk // side
    for row in range(side):
        piece = total.at[row * rows : (row + 1) * rows, :]
        store_for(row, unit_row, piece, dict(enumerate(outs)))


def late_pieces(layout, own, arrived):
    side = layout.side
    chunk, width = own.shape
    rows = chunk // side
    vmem = pl.BlockSpec(memory_space=pltpu.VMEM)
    return pl.pallas_call(
        functools.partial(late_kernel, side, layout.mp),
        out_shape=[jax.ShapeDtypeStruct((rows, width), F32)]
        + [jax.ShapeDtypeStruct((rows, width), BF16)] * (side - 1),
        in_specs=[vmem] * 2,
        out_specs=[vmem] * side,
        scratch_shapes=[pltpu.VMEM((chunk, width), F32)],
        compiler_params=pltpu.CompilerParams(vmem_limit_bytes=12 * 1024 * 1024),
        name="late",
    )(own, arrived)


def per_device(layout, image_feats, text_feats, image_proj, text_proj, log_scale, logit_bias):
    side = layout.side
    own_rows, width = image_feats.shape
    devices = layout.dp * layout.mp
    out_rows = width // devices
    batch_total = own_rows * devices
    is_image = lax.axis_index("dp") % 2 == 0

    scalars = jnp.concatenate([jnp.exp(log_scale), logit_bias])

    images, texts, swapped, projected = {0: image_feats}, {0: text_feats}, {}, {}

    def swap(t):
        swapped[t] = layout.sibling(images[t]), layout.sibling(texts[t])

    def project_next(t):
        shards = [images[t], texts[t], *swapped[t]]
        projected[t] = project_chunk(image_proj, text_proj, shards, t == 0)

    last = side - 1
    bit = side // 2
    while bit > 1:
        for t in list(images):
            images[t ^ bit] = layout.along_row(images[t], bit)
            texts[t ^ bit] = layout.along_column(texts[t], bit)
        bit //= 2
    sources = [t for t in images if t]
    images[1] = layout.along_row(image_feats, 1)
    texts[1] = layout.along_column(text_feats, 1)
    swap(0)
    project_next(0)
    images, texts, projected = lax.optimization_barrier((images, texts, projected))
    for t in sources:
        images[t ^ 1] = layout.along_row(images[t], 1)
        texts[t ^ 1] = layout.along_column(texts[t], 1)
    for t in range(1, last):
        swap(t)
        project_next(t)
    images[last], texts[last], projected = lax.optimization_barrier(
        (images[last], texts[last], projected)
    )
    swap(last)
    groups = ((0, 512), (512, 896))
    results = block_grads(
        layout,
        groups,
        scalars,
        image_proj,
        text_proj,
        [images[last], texts[last], *swapped[last]],
        [projected[t] for t in range(last)],
    )
    count = side * len(groups)
    firsts = [list(results[g : g + side]) for g in range(0, count, side)]
    late, message, stats = results[count:]

    bit = side // 2
    arrived = layout.along_row(message, bit)
    for g, group in enumerate(firsts):
        if g:
            group[1:], firsts[g - 1][1] = lax.optimization_barrier((group[1:], firsts[g - 1][1]))
        group[1:] = [layout.along_column(group[t], t) for t in range(1, side)]
    while bit > 1:
        late, message = halve(late, arrived)
        bit //= 2
        arrived = layout.along_row(message, bit)

    for g, group in enumerate(firsts):
        own_stats = None if g else stats
        pieces = list(first_pieces(layout, group[0], own_stats, group[1:]))
        if not g:
            stats = pieces.pop()
        group[:] = [pieces[0]] + [layout.along_row(pieces[t], t) for t in range(1, side)]
    lates = list(late_pieces(layout, late, arrived))
    lates[1:] = [layout.along_column(lates[t], t) for t in range(1, side)]
    firsts, lates = lax.optimization_barrier((firsts, lates))
    last_rows = 2 * out_rows
    sums = [tree_sum([x[:last_rows].astype(F32) for x in group]) for group in [*firsts, lates]]
    total = jnp.concatenate(sums, axis=1)
    parts = [x[-8:-5, :384].astype(F32) for x in firsts[0][1:]]
    stat_total = tree_sum([stats[0]] + [x[0] + x[1] + x[2] for x in parts])

    upper, lower = total[:out_rows], total[out_rows:]
    keep, give = jnp.where(is_image, upper, lower), jnp.where(is_image, lower, upper)
    got = layout.sibling(give)
    image_proj_grad = jnp.where(is_image, keep, got)
    text_proj_grad = jnp.where(is_image, got, keep)
    stat_total = stat_total + layout.sibling(stat_total)
    totals = jnp.sum(stat_total.reshape(3, 128), axis=1) * (0.5 / batch_total)
    return totals[0:1], image_proj_grad, text_proj_grad, totals[1:2], totals[2:3]


def solution(mesh):
    layout = Layout(mesh.shape["dp"], mesh.shape["mp"])
    return jax.shard_map(
        functools.partial(per_device, layout),
        mesh=mesh,
        in_specs=(P(AXES, None), P(AXES, None), P(), P(), P(), P()),
        out_specs=(P(), P(AXES, None), P(AXES, None), P(), P()),
        check_vma=False,
    )
```

```python
import functools
import math

import jax
import jax.numpy as jnp
from jax import lax
from jax.experimental import pallas as pl
from jax.experimental.pallas import tpu as pltpu
from jax.sharding import PartitionSpec as P

F32 = jnp.float32
BF16 = jnp.bfloat16
AXES = ("dp", "mp")


class Layout:
    def __init__(self, dp_size, mp_size):
        self.dp, self.mp = dp_size, mp_size
        self.units = dp_size * mp_size // 2
        self.side = math.isqrt(self.units)
        if self.side * self.side != self.units or self.side % mp_size or self.side & (self.side - 1):
            raise ValueError("unsupported mesh")

    def device(self, unit, core):
        return (2 * (unit // self.mp) + core) * self.mp + unit % self.mp

    def send(self, value, step):
        s = self.side
        pairs = []
        for unit in range(self.units):
            for core in range(2):
                row, column, other = step(*divmod(unit, s), core)
                pairs.append((self.device(unit, core), self.device(row * s + column, other)))
        return lax.ppermute(value, AXES, pairs)

    def along_column(self, value, t):
        return self.send(value, lambda r, c, core: (r ^ t, c, core))

    def along_row(self, value, t):
        return self.send(value, lambda r, c, core: (r, c ^ t, core))

    def exchange(self, value, row_bits, column_bits):
        return self.send(value, lambda r, c, core: (r ^ row_bits, c ^ column_bits, core))

    def sibling(self, value):
        return self.send(value, lambda r, c, core: (r, c, 1 - core))


def tree_sum(values):
    values = list(values)
    while len(values) > 1:
        values = [a + b for a, b in zip(values[::2], values[1::2])]
    return values[0]


def this_core():
    return lax.rem(lax.axis_index("dp"), 2)


def load_projections(image_proj, text_proj, projs, sems):
    core = this_core()
    own = pltpu.make_async_copy(image_proj, projs.at[core], sems.at[0])
    other = pltpu.make_async_copy(text_proj, projs.at[1 - core], sems.at[1])
    own.start()
    other.start()
    return [own, other]


def load_chunk(shards, feats, sems):
    core = this_core()
    rows = shards[0].shape[0]
    copies = []
    for i, shard in enumerate(shards):
        place = pl.ds((core if i < 2 else 1 - core) * rows, rows)
        side = core if i % 2 == 0 else 1 - core
        copies.append(pltpu.make_async_copy(shard, feats.at[side, place], sems.at[i]))
        copies[-1].start()
    return copies


def project(rows, projection):
    raw = jnp.dot(rows, projection, preferred_element_type=F32)
    inverse = lax.rsqrt(jnp.sum(raw * raw, axis=-1, keepdims=True) + 1e-06)
    return raw * inverse, inverse


def project_kernel(image_proj, text_proj, *refs):
    shards, (own_chunk, own_unit, own_inverse, other_half, feats, projs, sems) = refs[:4], refs[4:]
    copies = load_chunk(shards, feats, sems.at[pl.ds(2, 4)])
    copies += load_projections(image_proj, text_proj, projs, sems.at[pl.ds(0, 2)])
    for copy in copies:
        copy.wait()
    unit, _ = project(feats[1], projs[1])
    other_half[...] = unit.astype(BF16)
    unit, inverse = project(feats[0], projs[0])
    own_unit[...] = unit
    own_inverse[...] = jnp.broadcast_to(inverse, own_inverse.shape)
    own_chunk[...] = feats[0]


def project_chunk(image_proj, text_proj, shards, from_arguments):
    rows, width = shards[0].shape
    rows = 2 * rows
    anywhere = pl.BlockSpec(memory_space=pl.ANY)
    hbm = pl.BlockSpec(memory_space=pltpu.HBM)
    vmem = pl.BlockSpec(memory_space=pltpu.VMEM)
    return pl.pallas_call(
        project_kernel,
        out_shape=[
            jax.ShapeDtypeStruct((rows, width), BF16),
            jax.ShapeDtypeStruct((rows, width), F32),
            jax.ShapeDtypeStruct((rows, 128), F32),
            jax.ShapeDtypeStruct((rows, width), BF16),
        ],
        in_specs=[hbm] * 2 + [hbm if from_arguments else anywhere] * 2 + [anywhere] * 2,
        out_specs=[vmem] * 4,
        scratch_shapes=[
            pltpu.VMEM((2, rows, width), BF16),
            pltpu.VMEM((2, width, width), BF16),
            pltpu.SemaphoreType.DMA((6,)),
        ],
        compiler_params=pltpu.CompilerParams(
            vmem_limit_bytes=4 * width * width + 24 * rows * width + 4 * 1024 * 1024
        ),
        cost_estimate=pl.CostEstimate(
            flops=4 * rows * width * width,
            bytes_accessed=4 * width * width + 12 * rows * width,
            transcendentals=2 * rows,
        ),
        name="project",
    )(image_proj, text_proj, *shards)


def pair_terms(cosine, scale, bias, masked):
    logits = scale * cosine + bias
    raised = jnp.exp(logits)
    total = 1.0 + raised
    inverse = 1.0 / total
    losses = jnp.log(total) + (raised - (total - 1.0)) * inverse
    pair_grads = raised * inverse
    if masked:
        equal = lax.broadcasted_iota(jnp.int32, cosine.shape, 0) == lax.broadcasted_iota(
            jnp.int32, cosine.shape, 1
        )
        losses = jnp.where(equal, jnp.log1p(jnp.exp(-logits)), losses)
        pair_grads = jnp.where(equal, -inverse, pair_grads)
    return losses, pair_grads


def lane_sums(values):
    total = jnp.sum(values, axis=0, keepdims=True)
    return sum(total[:, j : j + 128] for j in range(0, total.shape[1], 128))


def block_kernel(side, mp_size, scalars, image_proj, text_proj, *refs):
    last_shards, refs = refs[:4], refs[4:]
    own_chunks, refs = refs[: side - 1], refs[side - 1 :]
    own_units, refs = refs[: side - 1], refs[side - 1 :]
    own_inverses, refs = refs[: side - 1], refs[side - 1 :]
    other_halves, refs = refs[: side - 1], refs[side - 1 :]
    orders = part_orders(side)
    results, refs = refs[: 2 * len(orders)], refs[2 * len(orders) :]
    stats, projs, last, feats, units, inverses, other_half, dy, grad, pieces, moving, sems = refs
    rows, width = dy.shape
    chunk_rows = rows // side
    rest = rows - chunk_rows
    dp_index, mp_index = lax.axis_index("dp"), lax.axis_index("mp")
    unit_index = dp_index // 2 * mp_size + mp_index
    unit_row, unit_column = unit_index // side, lax.rem(unit_index, side)
    scale, bias = scalars[0], scalars[1]

    count = 6

    def start(source, target):
        nonlocal count
        copy = pltpu.make_async_copy(source, target, sems.at[count])
        copy.start()
        count += 1
        return copy

    def places(i):
        return pl.ds(i * chunk_rows, chunk_rows)

    first_copies = load_chunk(last_shards, last, sems.at[pl.ds(2, 4)])
    first_copies += load_projections(image_proj, text_proj, projs, sems.at[pl.ds(0, 2)])
    other_copies = [start(other_halves[i], other_half.at[places(i)]) for i in range(side - 1)]
    unit_copies = [start(own_units[i], units.at[places(i)]) for i in range(side - 1)]
    unit_copies += [start(own_inverses[i], inverses.at[places(i)]) for i in range(side - 1)]
    feat_copies = [start(own_chunks[i], feats.at[places(i)]) for i in range(side - 1)]

    for copy in first_copies:
        copy.wait()
    unit, _ = project(last[1], projs[1])
    other_half[rest:, :] = unit.astype(BF16)
    unit, inverse = project(last[0], projs[0])
    units[rest:, :] = unit
    inverses[rest:, :] = jnp.broadcast_to(inverse, (chunk_rows, 128))
    feats[rest:, :] = last[0]
    for copy in other_copies + unit_copies:
        copy.wait()

    def cosines(i):
        half = units[i * chunk_rows : (i + 1) * chunk_rows, :].astype(BF16)
        return lax.dot_general(
            half, other_half[...], (((1,), (1,)), ((), ())), preferred_element_type=F32
        )

    total = None
    cosine = cosines(0)
    for i in range(side):
        following = cosines(i + 1) if i + 1 < side else None
        if i == 0:
            terms = [
                pair_terms(cosine[:, :chunk_rows], scale, bias, True),
                pair_terms(cosine[:, chunk_rows:], scale, bias, False),
            ]
            losses, pair_grads = [jnp.concatenate(x, axis=1) for x in zip(*terms)]
        else:
            losses, pair_grads = pair_terms(cosine, scale, bias, False)
        half_grads = pair_grads.astype(BF16)
        sums = [lane_sums(losses), lane_sums(pair_grads * cosine) * scale, lane_sums(pair_grads)]
        sums = jnp.concatenate(sums, axis=1)
        total = sums if total is None else total + sums
        inner = jnp.sum(half_grads.astype(F32) * cosine, axis=-1, keepdims=True)
        grads = jnp.dot(half_grads, other_half[...], preferred_element_type=F32)
        place = slice(i * chunk_rows, (i + 1) * chunk_rows)
        grads = (grads - units[place, :] * inner) * (scale * inverses[place, 0:1])
        dy[place, :] = grads.astype(BF16)
        cosine = following
    stats[0:1, :] = total

    for copy in feat_copies:
        copy.wait()
    for j in range(0, width, 128):
        grad[j : j + 128, :] = lax.dot_general(
            feats[:, j : j + 128], dy[...], (((0,), (0,)), ((), ())), preferred_element_type=F32
        )

    sums = stats[0:1, :]
    stats[...] = jnp.broadcast_to(sums, stats.shape)
    chunk = width // side
    out_rows = chunk // (2 * side)
    piece_rows = pieces.shape[0] // side**2
    for unit in range(side**2):
        row, column = divmod(unit, side)
        for core in range(2):
            source = row * chunk + shard_of(column, core, mp_size) * out_rows
            target = unit * piece_rows + core * out_rows
            pieces[target : target + out_rows, :] = grad[source : source + out_rows, :]
        if piece_rows > 2 * out_rows:
            target = unit * piece_rows + 2 * out_rows
            pieces[target : (unit + 1) * piece_rows, :] = jnp.zeros(
                (piece_rows - 2 * out_rows, width), F32
            )
    half = side**2 // 2
    part_width = width // len(orders)
    moving[half * piece_rows :, :] = stat_rows(sums, part_width)
    for g, order in enumerate(orders):
        own, message = results[2 * g : 2 * g + 2]
        columns = slice(g * part_width, (g + 1) * part_width)
        for p in range(2 * half):
            row, column = relative_unit(order, p)
            unit = jnp.bitwise_xor(unit_row, row) * side + jnp.bitwise_xor(unit_column, column)
            block = pieces[pl.ds(pl.multiple_of(unit * piece_rows, 8), piece_rows), columns]
            target = p % half * piece_rows
            (own if p < half else moving)[target : target + piece_rows, :] = block
        message[...] = moving[: message.shape[0], :].astype(BF16)


def part_orders(side):
    bits = [1 << i for i in range(side.bit_length() - 1)]
    rows, columns = [(b, 0) for b in bits], [(0, b) for b in bits]
    return [
        rows + columns[::-1],
        [rows[-1], columns[0]] + rows[:-1] + columns[1:],
        [columns[0]] + rows + columns[1:],
    ]


def relative_unit(order, position):
    row = column = 0
    for i, step in enumerate(reversed(order)):
        if position >> i & 1:
            row, column = row | step[0], column | step[1]
    return row, column


def shard_of(column, core, mp_size):
    return column // mp_size * 2 * mp_size + core * mp_size + column % mp_size


def stat_rows(sums, width):
    part0 = sums.astype(BF16).astype(F32)
    part1 = (sums - part0).astype(BF16).astype(F32)
    part2 = sums - part0 - part1
    line = lax.broadcasted_iota(jnp.int32, (8, sums.shape[1]), 0)
    parts = jnp.where(line == 0, part0, jnp.where(line == 1, part1, jnp.where(line == 2, part2, 0.0)))
    if width > sums.shape[1]:
        parts = jnp.concatenate([parts, jnp.zeros((8, width - sums.shape[1]), F32)], axis=1)
    return parts


def block_grads(layout, scalars, image_proj, text_proj, last_shards, projected):
    side = layout.side
    chunk_rows, width = projected[0][0].shape
    rows = side * chunk_rows
    anywhere = pl.BlockSpec(memory_space=pl.ANY)
    vmem = pl.BlockSpec(memory_space=pltpu.VMEM)
    operands = [image_proj, text_proj, *last_shards]
    operands += [x for column in zip(*projected) for x in column]
    parts = len(part_orders(side))
    part_width = width // parts
    piece_rows = (width // layout.units + 7) // 8 * 8
    half_rows = layout.units // 2 * piece_rows
    out_shape = []
    for g in range(parts):
        out_shape.append(jax.ShapeDtypeStruct((half_rows, part_width), F32))
        out_shape.append(jax.ShapeDtypeStruct((half_rows if g else half_rows + 8, part_width), BF16))
    out_shape.append(jax.ShapeDtypeStruct((8, part_width), F32))
    needed = 6 * width * width + 14 * rows * width + 16 * half_rows * width
    needed += 12 * chunk_rows * rows + 2 * 1024 * 1024
    return pl.pallas_call(
        functools.partial(block_kernel, side, layout.mp),
        out_shape=out_shape,
        in_specs=[pl.BlockSpec(memory_space=pltpu.SMEM)]
        + [pl.BlockSpec(memory_space=pltpu.HBM)] * 2
        + [anywhere] * (len(operands) - 2),
        out_specs=[vmem] * len(out_shape),
        scratch_shapes=[
            pltpu.VMEM((2, width, width), BF16),
            pltpu.VMEM((2, chunk_rows, width), BF16),
            pltpu.VMEM((rows, width), BF16),
            pltpu.VMEM((rows, width), F32),
            pltpu.VMEM((rows, 128), F32),
            pltpu.VMEM((rows, width), BF16),
            pltpu.VMEM((rows, width), BF16),
            pltpu.VMEM((width, width), F32),
            pltpu.VMEM((2 * half_rows, width), F32),
            pltpu.VMEM((half_rows + 8, part_width), F32),
            pltpu.SemaphoreType.DMA((len(operands),)),
        ],
        compiler_params=pltpu.CompilerParams(vmem_limit_bytes=min(needed, 60 * 1024 * 1024)),
        cost_estimate=pl.CostEstimate(
            flops=2 * rows * width * (2 * rows + width) + 4 * chunk_rows * width * width,
            bytes_accessed=12 * rows * width + 4 * width * width,
            transcendentals=3 * rows * rows,
        ),
        name="block",
    )(scalars, *operands)


def halve_kernel(own, arrived, *refs):
    rows, half = own.shape[0], own.shape[0] // 2
    total = arrived[...].astype(F32)
    keep, message = refs[-2], refs[-1]
    moved = own[half:, :] + total[half:rows, :]
    keep[...] = own[:half, :] + total[:half, :]
    if len(refs) > 2:
        own_stats, stats = refs[0], refs[1]
        parts = total[rows:, :]
        sums = own_stats[0:1, :] + (parts[0:1, :] + parts[1:2, :] + parts[2:3, :])
        stats[...] = jnp.broadcast_to(sums, stats.shape)
        moved = jnp.concatenate([moved, stat_rows(sums, own.shape[1])], axis=0)
    message[...] = moved.astype(BF16)


def halve(own, arrived, *own_stats):
    rows, width = own.shape
    half = rows // 2
    vmem = pl.BlockSpec(memory_space=pltpu.VMEM)
    stats = [jax.ShapeDtypeStruct(x.shape, F32) for x in own_stats]
    out_shape = [
        *stats,
        jax.ShapeDtypeStruct((half, width), F32),
        jax.ShapeDtypeStruct((half + 8 * len(stats), width), BF16),
    ]
    return pl.pallas_call(
        halve_kernel,
        out_shape=out_shape,
        in_specs=[vmem] * (2 + len(stats)),
        out_specs=[vmem] * len(out_shape),
        compiler_params=pltpu.CompilerParams(vmem_limit_bytes=12 * 1024 * 1024),
        name="halve",
    )(own, arrived, *own_stats)


def per_device(layout, image_feats, text_feats, image_proj, text_proj, log_scale, logit_bias):
    side = layout.side
    own_rows, width = image_feats.shape
    devices = layout.dp * layout.mp
    out_rows = width // devices
    batch_total = own_rows * devices
    is_image = lax.axis_index("dp") % 2 == 0

    scalars = jnp.concatenate([jnp.exp(log_scale), logit_bias])

    images, texts, swapped, projected = {0: image_feats}, {0: text_feats}, {}, {}

    def swap(t):
        swapped[t] = layout.sibling(images[t]), layout.sibling(texts[t])

    def project_next(t):
        shards = [images[t], texts[t], *swapped[t]]
        projected[t] = project_chunk(image_proj, text_proj, shards, t == 0)

    last = side - 1
    bit = side // 2
    while bit > 1:
        for t in list(images):
            images[t ^ bit] = layout.along_row(images[t], bit)
            texts[t ^ bit] = layout.along_column(texts[t], bit)
        bit //= 2
    sources = [t for t in images if t]
    images[1] = layout.along_row(image_feats, 1)
    texts[1] = layout.along_column(text_feats, 1)
    swap(0)
    project_next(0)
    images, texts, projected = lax.optimization_barrier((images, texts, projected))
    for t in sources:
        images[t ^ 1] = layout.along_row(images[t], 1)
        texts[t ^ 1] = layout.along_column(texts[t], 1)
    for t in range(1, last):
        swap(t)
        project_next(t)
    images[last], texts[last], projected = lax.optimization_barrier(
        (images[last], texts[last], projected)
    )
    swap(last)
    results = block_grads(
        layout,
        scalars,
        image_proj,
        text_proj,
        [images[last], texts[last], *swapped[last]],
        [projected[t] for t in range(last)],
    )
    orders = part_orders(side)
    owns, messages = list(results[0:-1:2]), list(results[1:-1:2])
    stats = [results[-1]]

    steps = len(orders[0])
    for step in range(steps):
        arrived = [
            layout.exchange(message, *order[step]) for message, order in zip(messages, orders)
        ]
        if step + 1 < steps:
            for g in range(len(orders)):
                *some, owns[g], messages[g] = halve(owns[g], arrived[g], *([] if g else stats))
                stats = some if g == 0 else stats
    last_rows = 2 * out_rows
    total = jnp.concatenate(
        [own[:last_rows] + x[:last_rows].astype(F32) for own, x in zip(owns, arrived)], axis=1
    )
    parts = arrived[0][owns[0].shape[0] :].astype(F32)
    stat_total = stats[0][0] + (parts[0] + parts[1] + parts[2])

    upper, lower = total[:out_rows], total[out_rows:]
    keep, give = jnp.where(is_image, upper, lower), jnp.where(is_image, lower, upper)
    got = layout.sibling(give)
    image_proj_grad = jnp.where(is_image, keep, got)
    text_proj_grad = jnp.where(is_image, got, keep)
    stat_total = stat_total + layout.sibling(stat_total)
    totals = jnp.sum(stat_total.reshape(3, 128), axis=1) * (0.5 / batch_total)
    return totals[0:1], image_proj_grad, text_proj_grad, totals[1:2], totals[2:3]


def solution(mesh):
    layout = Layout(mesh.shape["dp"], mesh.shape["mp"])
    return jax.shard_map(
        functools.partial(per_device, layout),
        mesh=mesh,
        in_specs=(P(AXES, None), P(AXES, None), P(), P(), P(), P()),
        out_specs=(P(), P(AXES, None), P(AXES, None), P(), P()),
        check_vma=False,
    )
```

```python
import functools
import math

import jax
import jax.numpy as jnp
from jax import lax
from jax.experimental import pallas as pl
from jax.experimental.pallas import tpu as pltpu
from jax.sharding import PartitionSpec as P

F32 = jnp.float32
BF16 = jnp.bfloat16
AXES = ("dp", "mp")


class Layout:
    def __init__(self, dp_size, mp_size):
        self.dp, self.mp = dp_size, mp_size
        self.units = dp_size * mp_size // 2
        self.side = math.isqrt(self.units)
        if self.side * self.side != self.units or self.side % mp_size or self.side & (self.side - 1):
            raise ValueError("unsupported mesh")

    def device(self, unit, core):
        return (2 * (unit // self.mp) + core) * self.mp + unit % self.mp

    def send(self, value, step):
        s = self.side
        pairs = []
        for unit in range(self.units):
            for core in range(2):
                row, column, other = step(*divmod(unit, s), core)
                pairs.append((self.device(unit, core), self.device(row * s + column, other)))
        return lax.ppermute(value, AXES, pairs)

    def along_column(self, value, t):
        return self.send(value, lambda r, c, core: (r ^ t, c, core))

    def along_row(self, value, t):
        return self.send(value, lambda r, c, core: (r, c ^ t, core))

    def exchange(self, value, row_bits, column_bits):
        return self.send(value, lambda r, c, core: (r ^ row_bits, c ^ column_bits, core))

    def sibling(self, value):
        return self.send(value, lambda r, c, core: (r, c, 1 - core))


def tree_sum(values):
    values = list(values)
    while len(values) > 1:
        values = [a + b for a, b in zip(values[::2], values[1::2])]
    return values[0]


def this_core():
    return lax.rem(lax.axis_index("dp"), 2)


def by_role(image_proj, text_proj, body):
    core = this_core()

    @pl.when(core == 0)
    def _():
        body(image_proj, text_proj)

    @pl.when(core == 1)
    def _():
        body(text_proj, image_proj)


def load_chunk(shards, feats, sems):
    core = this_core()
    rows = shards[0].shape[0]
    copies = []
    for i, shard in enumerate(shards):
        place = pl.ds((core if i < 2 else 1 - core) * rows, rows)
        side = core if i % 2 == 0 else 1 - core
        copies.append(pltpu.make_async_copy(shard, feats.at[side, place], sems.at[i]))
        copies[-1].start()
    return copies


def project(rows, projection):
    raw = jnp.dot(rows, projection, preferred_element_type=F32)
    inverse = lax.rsqrt(jnp.sum(raw * raw, axis=-1, keepdims=True) + 1e-06)
    return raw * inverse, inverse


def project_kernel(image_proj, text_proj, *refs):
    shards, (own_chunk, own_unit, own_inverse, other_half, feats, sems) = refs[:4], refs[4:]
    for copy in load_chunk(shards, feats, sems):
        copy.wait()

    def body(own_proj, other_proj):
        unit, _ = project(feats[1], other_proj[...])
        other_half[...] = unit.astype(BF16)
        unit, inverse = project(feats[0], own_proj[...])
        own_unit[...] = unit
        own_inverse[...] = jnp.broadcast_to(inverse, own_inverse.shape)

    by_role(image_proj, text_proj, body)
    own_chunk[...] = feats[0]


def project_chunk(image_proj, text_proj, shards, from_arguments):
    rows, width = shards[0].shape
    rows = 2 * rows
    anywhere = pl.BlockSpec(memory_space=pl.ANY)
    hbm = pl.BlockSpec(memory_space=pltpu.HBM)
    vmem = pl.BlockSpec(memory_space=pltpu.VMEM)
    return pl.pallas_call(
        project_kernel,
        out_shape=[
            jax.ShapeDtypeStruct((rows, width), BF16),
            jax.ShapeDtypeStruct((rows, width), F32),
            jax.ShapeDtypeStruct((rows, 128), F32),
            jax.ShapeDtypeStruct((rows, width), BF16),
        ],
        in_specs=[vmem] * 2 + [hbm if from_arguments else anywhere] * 2 + [anywhere] * 2,
        out_specs=[vmem] * 4,
        scratch_shapes=[
            pltpu.VMEM((2, rows, width), BF16),
            pltpu.SemaphoreType.DMA((4,)),
        ],
        compiler_params=pltpu.CompilerParams(
            vmem_limit_bytes=4 * width * width + 24 * rows * width + 4 * 1024 * 1024
        ),
        cost_estimate=pl.CostEstimate(
            flops=4 * rows * width * width,
            bytes_accessed=4 * width * width + 12 * rows * width,
            transcendentals=2 * rows,
        ),
        name="project",
    )(image_proj, text_proj, *shards)


def pair_terms(cosine, scale, bias, masked):
    logits = scale * cosine + bias
    raised = jnp.exp(logits)
    total = 1.0 + raised
    inverse = 1.0 / total
    losses = jnp.log(total) + (raised - (total - 1.0)) * inverse
    pair_grads = raised * inverse
    if masked:
        equal = lax.broadcasted_iota(jnp.int32, cosine.shape, 0) == lax.broadcasted_iota(
            jnp.int32, cosine.shape, 1
        )
        losses = jnp.where(equal, jnp.log1p(jnp.exp(-logits)), losses)
        pair_grads = jnp.where(equal, -inverse, pair_grads)
    return losses, pair_grads


def lane_sums(values):
    total = jnp.sum(values, axis=0, keepdims=True)
    return sum(total[:, j : j + 128] for j in range(0, total.shape[1], 128))


def block_kernel(side, mp_size, scalars, image_proj, text_proj, *refs):
    last_shards, refs = refs[:4], refs[4:]
    own_chunks, refs = refs[: side - 1], refs[side - 1 :]
    own_units, refs = refs[: side - 1], refs[side - 1 :]
    own_inverses, refs = refs[: side - 1], refs[side - 1 :]
    other_halves, refs = refs[: side - 1], refs[side - 1 :]
    orders = part_orders(side)
    results, refs = refs[: 2 * len(orders)], refs[2 * len(orders) :]
    stats, last, feats, units, inverses, other_half, dy, grad, pieces, moving, sems = refs
    rows, width = dy.shape
    chunk_rows = rows // side
    rest = rows - chunk_rows
    dp_index, mp_index = lax.axis_index("dp"), lax.axis_index("mp")
    unit_index = dp_index // 2 * mp_size + mp_index
    unit_row, unit_column = unit_index // side, lax.rem(unit_index, side)
    scale, bias = scalars[0], scalars[1]

    count = 4

    def start(source, target):
        nonlocal count
        copy = pltpu.make_async_copy(source, target, sems.at[count])
        copy.start()
        count += 1
        return copy

    def places(i):
        return pl.ds(i * chunk_rows, chunk_rows)

    first_copies = load_chunk(last_shards, last, sems.at[pl.ds(0, 4)])
    other_copies = [start(other_halves[i], other_half.at[places(i)]) for i in range(side - 1)]
    unit_copies = [start(own_units[i], units.at[places(i)]) for i in range(side - 1)]
    unit_copies += [start(own_inverses[i], inverses.at[places(i)]) for i in range(side - 1)]
    feat_copies = [start(own_chunks[i], feats.at[places(i)]) for i in range(side - 1)]

    for copy in first_copies:
        copy.wait()

    def project_last(own_proj, other_proj):
        unit, _ = project(last[1], other_proj[...])
        other_half[rest:, :] = unit.astype(BF16)
        unit, inverse = project(last[0], own_proj[...])
        units[rest:, :] = unit
        inverses[rest:, :] = jnp.broadcast_to(inverse, (chunk_rows, 128))

    by_role(image_proj, text_proj, project_last)
    feats[rest:, :] = last[0]
    for copy in other_copies + unit_copies:
        copy.wait()

    def cosines(i):
        half = units[i * chunk_rows : (i + 1) * chunk_rows, :].astype(BF16)
        return lax.dot_general(
            half, other_half[...], (((1,), (1,)), ((), ())), preferred_element_type=F32
        )

    total = None
    cosine = cosines(0)
    for i in range(side):
        following = cosines(i + 1) if i + 1 < side else None
        if i == 0:
            terms = [
                pair_terms(cosine[:, :chunk_rows], scale, bias, True),
                pair_terms(cosine[:, chunk_rows:], scale, bias, False),
            ]
            losses, pair_grads = [jnp.concatenate(x, axis=1) for x in zip(*terms)]
        else:
            losses, pair_grads = pair_terms(cosine, scale, bias, False)
        half_grads = pair_grads.astype(BF16)
        sums = [lane_sums(losses), lane_sums(pair_grads * cosine) * scale, lane_sums(pair_grads)]
        sums = jnp.concatenate(sums, axis=1)
        total = sums if total is None else total + sums
        inner = jnp.sum(half_grads.astype(F32) * cosine, axis=-1, keepdims=True)
        grads = jnp.dot(half_grads, other_half[...], preferred_element_type=F32)
        place = slice(i * chunk_rows, (i + 1) * chunk_rows)
        grads = (grads - units[place, :] * inner) * (scale * inverses[place, 0:1])
        dy[place, :] = grads.astype(BF16)
        cosine = following
    stats[0:1, :] = total

    for copy in feat_copies:
        copy.wait()
    for j in range(0, width, 128):
        grad[j : j + 128, :] = lax.dot_general(
            feats[:, j : j + 128], dy[...], (((0,), (0,)), ((), ())), preferred_element_type=F32
        )

    sums = stats[0:1, :]
    stats[...] = jnp.broadcast_to(sums, stats.shape)
    chunk = width // side
    out_rows = chunk // (2 * side)
    piece_rows = pieces.shape[0] // side**2
    for unit in range(side**2):
        row, column = divmod(unit, side)
        for core in range(2):
            source = row * chunk + shard_of(column, core, mp_size) * out_rows
            target = unit * piece_rows + core * out_rows
            pieces[target : target + out_rows, :] = grad[source : source + out_rows, :]
        if piece_rows > 2 * out_rows:
            target = unit * piece_rows + 2 * out_rows
            pieces[target : (unit + 1) * piece_rows, :] = jnp.zeros(
                (piece_rows - 2 * out_rows, width), F32
            )
    half = side**2 // 2
    part_width = width // len(orders)
    moving[half * piece_rows :, :] = stat_rows(sums, part_width)
    for g, order in enumerate(orders):
        own, message = results[2 * g : 2 * g + 2]
        columns = slice(g * part_width, (g + 1) * part_width)
        for p in range(2 * half):
            row, column = relative_unit(order, p)
            unit = jnp.bitwise_xor(unit_row, row) * side + jnp.bitwise_xor(unit_column, column)
            block = pieces[pl.ds(pl.multiple_of(unit * piece_rows, 8), piece_rows), columns]
            target = p % half * piece_rows
            (own if p < half else moving)[target : target + piece_rows, :] = block
        message[...] = moving[: message.shape[0], :].astype(BF16)


def part_orders(side):
    bits = [1 << i for i in range(side.bit_length() - 1)]
    rows, columns = [(b, 0) for b in bits], [(0, b) for b in bits]
    return [
        rows + columns[::-1],
        [rows[-1], columns[0]] + rows[:-1] + columns[1:],
        [columns[0]] + rows + columns[1:],
    ]


def relative_unit(order, position):
    row = column = 0
    for i, step in enumerate(reversed(order)):
        if position >> i & 1:
            row, column = row | step[0], column | step[1]
    return row, column


def shard_of(column, core, mp_size):
    return column // mp_size * 2 * mp_size + core * mp_size + column % mp_size


def stat_rows(sums, width):
    part0 = sums.astype(BF16).astype(F32)
    part1 = (sums - part0).astype(BF16).astype(F32)
    part2 = sums - part0 - part1
    line = lax.broadcasted_iota(jnp.int32, (8, sums.shape[1]), 0)
    parts = jnp.where(line == 0, part0, jnp.where(line == 1, part1, jnp.where(line == 2, part2, 0.0)))
    if width > sums.shape[1]:
        parts = jnp.concatenate([parts, jnp.zeros((8, width - sums.shape[1]), F32)], axis=1)
    return parts


def block_grads(layout, scalars, image_proj, text_proj, last_shards, projected):
    side = layout.side
    chunk_rows, width = projected[0][0].shape
    rows = side * chunk_rows
    anywhere = pl.BlockSpec(memory_space=pl.ANY)
    vmem = pl.BlockSpec(memory_space=pltpu.VMEM)
    operands = [image_proj, text_proj, *last_shards]
    operands += [x for column in zip(*projected) for x in column]
    parts = len(part_orders(side))
    part_width = width // parts
    piece_rows = (width // layout.units + 7) // 8 * 8
    half_rows = layout.units // 2 * piece_rows
    out_shape = []
    for g in range(parts):
        out_shape.append(jax.ShapeDtypeStruct((half_rows, part_width), F32))
        out_shape.append(jax.ShapeDtypeStruct((half_rows if g else half_rows + 8, part_width), BF16))
    out_shape.append(jax.ShapeDtypeStruct((8, part_width), F32))
    needed = 6 * width * width + 14 * rows * width + 16 * half_rows * width
    needed += 12 * chunk_rows * rows + 2 * 1024 * 1024
    return pl.pallas_call(
        functools.partial(block_kernel, side, layout.mp),
        out_shape=out_shape,
        in_specs=[pl.BlockSpec(memory_space=pltpu.SMEM)]
        + [vmem] * 2
        + [anywhere] * (len(operands) - 2),
        out_specs=[vmem] * len(out_shape),
        scratch_shapes=[
            pltpu.VMEM((2, chunk_rows, width), BF16),
            pltpu.VMEM((rows, width), BF16),
            pltpu.VMEM((rows, width), F32),
            pltpu.VMEM((rows, 128), F32),
            pltpu.VMEM((rows, width), BF16),
            pltpu.VMEM((rows, width), BF16),
            pltpu.VMEM((width, width), F32),
            pltpu.VMEM((2 * half_rows, width), F32),
            pltpu.VMEM((half_rows + 8, part_width), F32),
            pltpu.SemaphoreType.DMA((len(operands) - 2,)),
        ],
        compiler_params=pltpu.CompilerParams(vmem_limit_bytes=min(needed, 60 * 1024 * 1024)),
        cost_estimate=pl.CostEstimate(
            flops=2 * rows * width * (2 * rows + width) + 4 * chunk_rows * width * width,
            bytes_accessed=12 * rows * width + 4 * width * width,
            transcendentals=3 * rows * rows,
        ),
        name="block",
    )(scalars, *operands)


def halve_kernel(own, arrived, *refs):
    rows, half = own.shape[0], own.shape[0] // 2
    total = arrived[...].astype(F32)
    keep, message = refs[-2], refs[-1]
    moved = own[half:, :] + total[half:rows, :]
    keep[...] = own[:half, :] + total[:half, :]
    if len(refs) > 2:
        own_stats, stats = refs[0], refs[1]
        parts = total[rows:, :]
        sums = own_stats[0:1, :] + (parts[0:1, :] + parts[1:2, :] + parts[2:3, :])
        stats[...] = jnp.broadcast_to(sums, stats.shape)
        moved = jnp.concatenate([moved, stat_rows(sums, own.shape[1])], axis=0)
    message[...] = moved.astype(BF16)


def halve(own, arrived, *own_stats):
    rows, width = own.shape
    half = rows // 2
    vmem = pl.BlockSpec(memory_space=pltpu.VMEM)
    stats = [jax.ShapeDtypeStruct(x.shape, F32) for x in own_stats]
    out_shape = [
        *stats,
        jax.ShapeDtypeStruct((half, width), F32),
        jax.ShapeDtypeStruct((half + 8 * len(stats), width), BF16),
    ]
    return pl.pallas_call(
        halve_kernel,
        out_shape=out_shape,
        in_specs=[vmem] * (2 + len(stats)),
        out_specs=[vmem] * len(out_shape),
        compiler_params=pltpu.CompilerParams(vmem_limit_bytes=12 * 1024 * 1024),
        name="halve",
    )(own, arrived, *own_stats)


def per_device(layout, image_feats, text_feats, image_proj, text_proj, log_scale, logit_bias):
    side = layout.side
    own_rows, width = image_feats.shape
    devices = layout.dp * layout.mp
    out_rows = width // devices
    batch_total = own_rows * devices
    is_image = lax.axis_index("dp") % 2 == 0

    scalars = jnp.concatenate([jnp.exp(log_scale), logit_bias])

    images, texts, swapped, projected = {0: image_feats}, {0: text_feats}, {}, {}

    def swap(t):
        swapped[t] = layout.sibling(images[t]), layout.sibling(texts[t])

    def project_next(t):
        shards = [images[t], texts[t], *swapped[t]]
        projected[t] = project_chunk(image_proj, text_proj, shards, t == 0)

    last = side - 1
    bit = side // 2
    while bit > 1:
        for t in list(images):
            images[t ^ bit] = layout.along_row(images[t], bit)
            texts[t ^ bit] = layout.along_column(texts[t], bit)
        bit //= 2
    sources = [t for t in images if t]
    images[1] = layout.along_row(image_feats, 1)
    texts[1] = layout.along_column(text_feats, 1)
    swap(0)
    project_next(0)
    images, texts, projected = lax.optimization_barrier((images, texts, projected))
    for t in sources:
        images[t ^ 1] = layout.along_row(images[t], 1)
        texts[t ^ 1] = layout.along_column(texts[t], 1)
    for t in range(1, last):
        swap(t)
        project_next(t)
    images[last], texts[last], projected = lax.optimization_barrier(
        (images[last], texts[last], projected)
    )
    swap(last)
    results = block_grads(
        layout,
        scalars,
        image_proj,
        text_proj,
        [images[last], texts[last], *swapped[last]],
        [projected[t] for t in range(last)],
    )
    orders = part_orders(side)
    owns, messages = list(results[0:-1:2]), list(results[1:-1:2])
    stats = [results[-1]]

    steps = len(orders[0])
    for step in range(steps):
        arrived = [
            layout.exchange(message, *order[step]) for message, order in zip(messages, orders)
        ]
        if step + 1 < steps:
            for g in range(len(orders)):
                *some, owns[g], messages[g] = halve(owns[g], arrived[g], *([] if g else stats))
                stats = some if g == 0 else stats
    last_rows = 2 * out_rows
    total = jnp.concatenate(
        [own[:last_rows] + x[:last_rows].astype(F32) for own, x in zip(owns, arrived)], axis=1
    )
    parts = arrived[0][owns[0].shape[0] :].astype(F32)
    stat_total = stats[0][0] + (parts[0] + parts[1] + parts[2])

    upper, lower = total[:out_rows], total[out_rows:]
    keep, give = jnp.where(is_image, upper, lower), jnp.where(is_image, lower, upper)
    got = layout.sibling(give)
    image_proj_grad = jnp.where(is_image, keep, got)
    text_proj_grad = jnp.where(is_image, got, keep)
    stat_total = stat_total + layout.sibling(stat_total)
    totals = jnp.sum(stat_total.reshape(3, 128), axis=1) * (0.5 / batch_total)
    return totals[0:1], image_proj_grad, text_proj_grad, totals[1:2], totals[2:3]


def solution(mesh):
    layout = Layout(mesh.shape["dp"], mesh.shape["mp"])
    return jax.shard_map(
        functools.partial(per_device, layout),
        mesh=mesh,
        in_specs=(P(AXES, None), P(AXES, None), P(), P(), P(), P()),
        out_specs=(P(), P(AXES, None), P(AXES, None), P(), P()),
        check_vma=False,
    )
```

```python
import functools
import math

import jax
import jax.numpy as jnp
from jax import lax
from jax.experimental import pallas as pl
from jax.experimental.pallas import tpu as pltpu
from jax.sharding import PartitionSpec as P

F32 = jnp.float32
BF16 = jnp.bfloat16
AXES = ("dp", "mp")


class Layout:
    def __init__(self, dp_size, mp_size):
        self.dp, self.mp = dp_size, mp_size
        self.units = dp_size * mp_size // 2
        self.side = math.isqrt(self.units)
        if self.side * self.side != self.units or self.side % mp_size or self.side & (self.side - 1):
            raise ValueError("unsupported mesh")

    def device(self, unit, core):
        return (2 * (unit // self.mp) + core) * self.mp + unit % self.mp

    def send(self, value, step):
        s = self.side
        pairs = []
        for unit in range(self.units):
            for core in range(2):
                row, column, other = step(*divmod(unit, s), core)
                pairs.append((self.device(unit, core), self.device(row * s + column, other)))
        return lax.ppermute(value, AXES, pairs)

    def along_column(self, value, t):
        return self.send(value, lambda r, c, core: (r ^ t, c, core))

    def along_row(self, value, t):
        return self.send(value, lambda r, c, core: (r, c ^ t, core))

    def exchange(self, value, row_bits, column_bits):
        return self.send(value, lambda r, c, core: (r ^ row_bits, c ^ column_bits, core))

    def sibling(self, value):
        return self.send(value, lambda r, c, core: (r, c, 1 - core))


def tree_sum(values):
    values = list(values)
    while len(values) > 1:
        values = [a + b for a, b in zip(values[::2], values[1::2])]
    return values[0]


def this_core():
    return lax.rem(lax.axis_index("dp"), 2)


def load_projections(image_proj, text_proj, projs, sems):
    core = this_core()
    own = pltpu.make_async_copy(image_proj, projs.at[core], sems.at[0])
    other = pltpu.make_async_copy(text_proj, projs.at[1 - core], sems.at[1])
    own.start()
    other.start()
    return [own, other]


def by_role(image_proj, text_proj, body):
    core = this_core()

    @pl.when(core == 0)
    def _():
        body(image_proj, text_proj)

    @pl.when(core == 1)
    def _():
        body(text_proj, image_proj)


def load_chunk(shards, feats, sems):
    core = this_core()
    rows = shards[0].shape[0]
    copies = []
    for i, shard in enumerate(shards):
        place = pl.ds((core if i < 2 else 1 - core) * rows, rows)
        side = core if i % 2 == 0 else 1 - core
        copies.append(pltpu.make_async_copy(shard, feats.at[side, place], sems.at[i]))
        copies[-1].start()
    return copies


def project(rows, projection):
    raw = jnp.dot(rows, projection, preferred_element_type=F32)
    inverse = lax.rsqrt(jnp.sum(raw * raw, axis=-1, keepdims=True) + 1e-06)
    return raw * inverse, inverse


def project_kernel(image_proj, text_proj, *refs):
    shards, (own_chunk, own_unit, own_inverse, other_half, feats, sems) = refs[:4], refs[4:]
    for copy in load_chunk(shards, feats, sems):
        copy.wait()

    def body(own_proj, other_proj):
        unit, _ = project(feats[1], other_proj[...])
        other_half[...] = unit.astype(BF16)
        unit, inverse = project(feats[0], own_proj[...])
        own_unit[...] = unit
        own_inverse[...] = jnp.broadcast_to(inverse, own_inverse.shape)

    by_role(image_proj, text_proj, body)
    own_chunk[...] = feats[0]


def project_chunk(image_proj, text_proj, shards, from_arguments):
    rows, width = shards[0].shape
    rows = 2 * rows
    anywhere = pl.BlockSpec(memory_space=pl.ANY)
    hbm = pl.BlockSpec(memory_space=pltpu.HBM)
    vmem = pl.BlockSpec(memory_space=pltpu.VMEM)
    return pl.pallas_call(
        project_kernel,
        out_shape=[
            jax.ShapeDtypeStruct((rows, width), BF16),
            jax.ShapeDtypeStruct((rows, width), F32),
            jax.ShapeDtypeStruct((rows, 128), F32),
            jax.ShapeDtypeStruct((rows, width), BF16),
        ],
        in_specs=[vmem] * 2 + [hbm if from_arguments else anywhere] * 2 + [anywhere] * 2,
        out_specs=[vmem] * 4,
        scratch_shapes=[
            pltpu.VMEM((2, rows, width), BF16),
            pltpu.SemaphoreType.DMA((4,)),
        ],
        compiler_params=pltpu.CompilerParams(
            vmem_limit_bytes=4 * width * width + 24 * rows * width + 4 * 1024 * 1024
        ),
        cost_estimate=pl.CostEstimate(
            flops=4 * rows * width * width,
            bytes_accessed=4 * width * width + 12 * rows * width,
            transcendentals=2 * rows,
        ),
        name="project",
    )(image_proj, text_proj, *shards)


def pair_terms(cosine, scale, bias, masked):
    logits = scale * cosine + bias
    raised = jnp.exp(logits)
    total = 1.0 + raised
    inverse = 1.0 / total
    losses = jnp.log(total) + (raised - (total - 1.0)) * inverse
    pair_grads = raised * inverse
    if masked:
        equal = lax.broadcasted_iota(jnp.int32, cosine.shape, 0) == lax.broadcasted_iota(
            jnp.int32, cosine.shape, 1
        )
        losses = jnp.where(equal, jnp.log1p(jnp.exp(-logits)), losses)
        pair_grads = jnp.where(equal, -inverse, pair_grads)
    return losses, pair_grads


def lane_sums(values):
    total = jnp.sum(values, axis=0, keepdims=True)
    return sum(total[:, j : j + 128] for j in range(0, total.shape[1], 128))


def block_kernel(side, mp_size, scalars, image_proj, text_proj, *refs):
    last_shards, refs = refs[:4], refs[4:]
    own_chunks, refs = refs[: side - 1], refs[side - 1 :]
    own_units, refs = refs[: side - 1], refs[side - 1 :]
    own_inverses, refs = refs[: side - 1], refs[side - 1 :]
    other_halves, refs = refs[: side - 1], refs[side - 1 :]
    orders = part_orders(side)
    results, refs = refs[: 2 * len(orders)], refs[2 * len(orders) :]
    stats, projs, last, feats, units, inverses, other_half, dy, grad, pieces, moving, sems = refs
    rows, width = dy.shape
    chunk_rows = rows // side
    rest = rows - chunk_rows
    dp_index, mp_index = lax.axis_index("dp"), lax.axis_index("mp")
    unit_index = dp_index // 2 * mp_size + mp_index
    unit_row, unit_column = unit_index // side, lax.rem(unit_index, side)
    scale, bias = scalars[0], scalars[1]

    count = 6

    def start(source, target):
        nonlocal count
        copy = pltpu.make_async_copy(source, target, sems.at[count])
        copy.start()
        count += 1
        return copy

    def places(i):
        return pl.ds(i * chunk_rows, chunk_rows)

    first_copies = load_chunk(last_shards, last, sems.at[pl.ds(2, 4)])
    first_copies += load_projections(image_proj, text_proj, projs, sems.at[pl.ds(0, 2)])
    other_copies = [start(other_halves[i], other_half.at[places(i)]) for i in range(side - 1)]
    unit_copies = [start(own_units[i], units.at[places(i)]) for i in range(side - 1)]
    unit_copies += [start(own_inverses[i], inverses.at[places(i)]) for i in range(side - 1)]
    feat_copies = [start(own_chunks[i], feats.at[places(i)]) for i in range(side - 1)]

    for copy in first_copies:
        copy.wait()
    unit, _ = project(last[1], projs[1])
    other_half[rest:, :] = unit.astype(BF16)
    unit, inverse = project(last[0], projs[0])
    units[rest:, :] = unit
    inverses[rest:, :] = jnp.broadcast_to(inverse, (chunk_rows, 128))
    feats[rest:, :] = last[0]
    for copy in other_copies + unit_copies:
        copy.wait()

    tile_rows = 2 * chunk_rows if rows <= 4 * chunk_rows else chunk_rows

    def cosines(i):
        half = units[i * tile_rows : (i + 1) * tile_rows, :].astype(BF16)
        return lax.dot_general(
            half, other_half[...], (((1,), (1,)), ((), ())), preferred_element_type=F32
        )

    total = None
    cosine = cosines(0)
    for i in range(rows // tile_rows):
        following = cosines(i + 1) if i + 1 < rows // tile_rows else None
        if i == 0:
            terms = [
                pair_terms(cosine[:, :chunk_rows], scale, bias, True),
                pair_terms(cosine[:, chunk_rows:], scale, bias, False),
            ]
            losses, pair_grads = [jnp.concatenate(x, axis=1) for x in zip(*terms)]
        else:
            losses, pair_grads = pair_terms(cosine, scale, bias, False)
        half_grads = pair_grads.astype(BF16)
        sums = [lane_sums(losses), lane_sums(pair_grads * cosine) * scale, lane_sums(pair_grads)]
        sums = jnp.concatenate(sums, axis=1)
        total = sums if total is None else total + sums
        inner = jnp.sum(half_grads.astype(F32) * cosine, axis=-1, keepdims=True)
        grads = jnp.dot(half_grads, other_half[...], preferred_element_type=F32)
        place = slice(i * tile_rows, (i + 1) * tile_rows)
        grads = (grads - units[place, :] * inner) * (scale * inverses[place, 0:1])
        dy[place, :] = grads.astype(BF16)
        cosine = following
    stats[0:1, :] = total

    for copy in feat_copies:
        copy.wait()
    for j in range(0, width, 128):
        grad[j : j + 128, :] = lax.dot_general(
            feats[:, j : j + 128], dy[...], (((0,), (0,)), ((), ())), preferred_element_type=F32
        )

    sums = stats[0:1, :]
    stats[...] = jnp.broadcast_to(sums, stats.shape)
    chunk = width // side
    out_rows = chunk // (2 * side)
    piece_rows = pieces.shape[0] // side**2
    for unit in range(side**2):
        row, column = divmod(unit, side)
        for core in range(2):
            source = row * chunk + shard_of(column, core, mp_size) * out_rows
            target = unit * piece_rows + core * out_rows
            pieces[target : target + out_rows, :] = grad[source : source + out_rows, :]
        if piece_rows > 2 * out_rows:
            target = unit * piece_rows + 2 * out_rows
            pieces[target : (unit + 1) * piece_rows, :] = jnp.zeros(
                (piece_rows - 2 * out_rows, width), F32
            )
    half = side**2 // 2
    part_width = width // len(orders)
    moving[half * piece_rows :, :] = stat_rows(sums, part_width)
    for g, order in enumerate(orders):
        own, message = results[2 * g : 2 * g + 2]
        columns = slice(g * part_width, (g + 1) * part_width)
        for p in range(2 * half):
            row, column = relative_unit(order, p)
            unit = jnp.bitwise_xor(unit_row, row) * side + jnp.bitwise_xor(unit_column, column)
            block = pieces[pl.ds(pl.multiple_of(unit * piece_rows, 8), piece_rows), columns]
            target = p % half * piece_rows
            (own if p < half else moving)[target : target + piece_rows, :] = block
        message[...] = moving[: message.shape[0], :].astype(BF16)


def part_orders(side):
    bits = [1 << i for i in range(side.bit_length() - 1)]
    rows, columns = [(b, 0) for b in bits], [(0, b) for b in bits]
    return [
        rows + columns[::-1],
        [rows[-1], columns[0]] + rows[:-1] + columns[1:],
        [columns[0]] + rows + columns[1:],
    ]


def relative_unit(order, position):
    row = column = 0
    for i, step in enumerate(reversed(order)):
        if position >> i & 1:
            row, column = row | step[0], column | step[1]
    return row, column


def shard_of(column, core, mp_size):
    return column // mp_size * 2 * mp_size + core * mp_size + column % mp_size


def stat_rows(sums, width):
    part0 = sums.astype(BF16).astype(F32)
    part1 = (sums - part0).astype(BF16).astype(F32)
    part2 = sums - part0 - part1
    line = lax.broadcasted_iota(jnp.int32, (8, sums.shape[1]), 0)
    parts = jnp.where(line == 0, part0, jnp.where(line == 1, part1, jnp.where(line == 2, part2, 0.0)))
    if width > sums.shape[1]:
        parts = jnp.concatenate([parts, jnp.zeros((8, width - sums.shape[1]), F32)], axis=1)
    return parts


def block_grads(layout, scalars, image_proj, text_proj, last_shards, projected):
    side = layout.side
    chunk_rows, width = projected[0][0].shape
    rows = side * chunk_rows
    anywhere = pl.BlockSpec(memory_space=pl.ANY)
    vmem = pl.BlockSpec(memory_space=pltpu.VMEM)
    operands = [image_proj, text_proj, *last_shards]
    operands += [x for column in zip(*projected) for x in column]
    parts = len(part_orders(side))
    part_width = width // parts
    piece_rows = (width // layout.units + 7) // 8 * 8
    half_rows = layout.units // 2 * piece_rows
    out_shape = []
    for g in range(parts):
        out_shape.append(jax.ShapeDtypeStruct((half_rows, part_width), F32))
        out_shape.append(jax.ShapeDtypeStruct((half_rows if g else half_rows + 8, part_width), BF16))
    out_shape.append(jax.ShapeDtypeStruct((8, part_width), F32))
    needed = 6 * width * width + 14 * rows * width + 16 * half_rows * width
    needed += 14 * chunk_rows * rows + 2 * 1024 * 1024
    return pl.pallas_call(
        functools.partial(block_kernel, side, layout.mp),
        out_shape=out_shape,
        in_specs=[pl.BlockSpec(memory_space=pltpu.SMEM)]
        + [pl.BlockSpec(memory_space=pltpu.HBM)] * 2
        + [anywhere] * (len(operands) - 2),
        out_specs=[vmem] * len(out_shape),
        scratch_shapes=[
            pltpu.VMEM((2, width, width), BF16),
            pltpu.VMEM((2, chunk_rows, width), BF16),
            pltpu.VMEM((rows, width), BF16),
            pltpu.VMEM((rows, width), F32),
            pltpu.VMEM((rows, 128), F32),
            pltpu.VMEM((rows, width), BF16),
            pltpu.VMEM((rows, width), BF16),
            pltpu.VMEM((width, width), F32),
            pltpu.VMEM((2 * half_rows, width), F32),
            pltpu.VMEM((half_rows + 8, part_width), F32),
            pltpu.SemaphoreType.DMA((len(operands),)),
        ],
        compiler_params=pltpu.CompilerParams(vmem_limit_bytes=min(needed, 60 * 1024 * 1024)),
        cost_estimate=pl.CostEstimate(
            flops=2 * rows * width * (2 * rows + width) + 4 * chunk_rows * width * width,
            bytes_accessed=12 * rows * width + 4 * width * width,
            transcendentals=3 * rows * rows,
        ),
        name="block",
    )(scalars, *operands)


def halve_kernel(own, arrived, *refs):
    rows, half = own.shape[0], own.shape[0] // 2
    total = arrived[...].astype(F32)
    keep, message = refs[-2], refs[-1]
    moved = own[half:, :] + total[half:rows, :]
    keep[...] = own[:half, :] + total[:half, :]
    if len(refs) > 2:
        own_stats, stats = refs[0], refs[1]
        parts = total[rows:, :]
        sums = own_stats[0:1, :] + (parts[0:1, :] + parts[1:2, :] + parts[2:3, :])
        stats[...] = jnp.broadcast_to(sums, stats.shape)
        moved = jnp.concatenate([moved, stat_rows(sums, own.shape[1])], axis=0)
    message[...] = moved.astype(BF16)


def halve_two_kernel(own_a, arrived_a, own_b, arrived_b, keep_a, keep_b, message):
    moved = []
    for own, arrived, keep in ((own_a, arrived_a, keep_a), (own_b, arrived_b, keep_b)):
        half = keep.shape[0]
        total = own[...] + arrived[...].astype(F32)
        keep[...] = total[:half, :]
        moved.append(total[half:, :])
    message[...] = jnp.concatenate(moved, axis=0).astype(BF16)


def halve_two(own_a, arrived_a, own_b, arrived_b):
    rows, width = own_a.shape
    vmem = pl.BlockSpec(memory_space=pltpu.VMEM)
    return pl.pallas_call(
        halve_two_kernel,
        out_shape=[jax.ShapeDtypeStruct((rows // 2, width), F32)] * 2
        + [jax.ShapeDtypeStruct((rows, width), BF16)],
        in_specs=[vmem] * 4,
        out_specs=[vmem] * 3,
        compiler_params=pltpu.CompilerParams(vmem_limit_bytes=12 * 1024 * 1024),
        name="halve_two",
    )(own_a, arrived_a, own_b, arrived_b)


def halve(own, arrived, *own_stats):
    rows, width = own.shape
    half = rows // 2
    vmem = pl.BlockSpec(memory_space=pltpu.VMEM)
    stats = [jax.ShapeDtypeStruct(x.shape, F32) for x in own_stats]
    out_shape = [
        *stats,
        jax.ShapeDtypeStruct((half, width), F32),
        jax.ShapeDtypeStruct((half + 8 * len(stats), width), BF16),
    ]
    return pl.pallas_call(
        halve_kernel,
        out_shape=out_shape,
        in_specs=[vmem] * (2 + len(stats)),
        out_specs=[vmem] * len(out_shape),
        compiler_params=pltpu.CompilerParams(vmem_limit_bytes=12 * 1024 * 1024),
        name="halve",
    )(own, arrived, *own_stats)


def per_device(layout, image_feats, text_feats, image_proj, text_proj, log_scale, logit_bias):
    side = layout.side
    own_rows, width = image_feats.shape
    devices = layout.dp * layout.mp
    out_rows = width // devices
    batch_total = own_rows * devices
    is_image = lax.axis_index("dp") % 2 == 0

    scalars = jnp.concatenate([jnp.exp(log_scale), logit_bias])

    images, texts, swapped, projected = {0: image_feats}, {0: text_feats}, {}, {}

    def swap(t):
        swapped[t] = layout.sibling(images[t]), layout.sibling(texts[t])

    def project_next(t):
        shards = [images[t], texts[t], *swapped[t]]
        projected[t] = project_chunk(image_proj, text_proj, shards, t == 0)

    last = side - 1
    bit = side // 2
    while bit > 1:
        for t in list(images):
            images[t ^ bit] = layout.along_row(images[t], bit)
            texts[t ^ bit] = layout.along_column(texts[t], bit)
        bit //= 2
    sources = [t for t in images if t]
    images[1] = layout.along_row(image_feats, 1)
    texts[1] = layout.along_column(text_feats, 1)
    swap(0)
    project_next(0)
    images, texts, projected = lax.optimization_barrier((images, texts, projected))
    for t in sources:
        images[t ^ 1] = layout.along_row(images[t], 1)
        texts[t ^ 1] = layout.along_column(texts[t], 1)
    for t in range(1, last):
        swap(t)
        project_next(t)
    images[last], texts[last], projected = lax.optimization_barrier(
        (images[last], texts[last], projected)
    )
    swap(last)
    results = block_grads(
        layout,
        scalars,
        image_proj,
        text_proj,
        [images[last], texts[last], *swapped[last]],
        [projected[t] for t in range(last)],
    )
    orders = part_orders(side)
    owns, messages = list(results[0:-1:2]), list(results[1:-1:2])
    stats = [results[-1]]

    steps = len(orders[0])
    for step in range(steps - 1):
        arrived = [
            layout.exchange(message, *order[step]) for message, order in zip(messages, orders)
        ]
        *stats, owns[0], messages[0] = halve(owns[0], arrived[0], *stats)
        if step + 2 < steps:
            for g in (1, 2):
                owns[g], messages[g] = halve(owns[g], arrived[g])
    owns[1], owns[2], message = halve_two(owns[1], arrived[1], owns[2], arrived[2])
    two = layout.exchange(message, *orders[1][-1])
    piece_rows = owns[1].shape[0]
    arrived = [layout.exchange(messages[0], *orders[0][-1]), two[:piece_rows], two[piece_rows:]]
    last_rows = 2 * out_rows
    total = jnp.concatenate(
        [own[:last_rows] + x[:last_rows].astype(F32) for own, x in zip(owns, arrived)], axis=1
    )
    parts = arrived[0][owns[0].shape[0] :].astype(F32)
    stat_total = stats[0][0] + (parts[0] + parts[1] + parts[2])

    upper, lower = total[:out_rows], total[out_rows:]
    keep, give = jnp.where(is_image, upper, lower), jnp.where(is_image, lower, upper)
    got = layout.sibling(give)
    image_proj_grad = jnp.where(is_image, keep, got)
    text_proj_grad = jnp.where(is_image, got, keep)
    stat_total = stat_total + layout.sibling(stat_total)
    totals = jnp.sum(stat_total.reshape(3, 128), axis=1) * (0.5 / batch_total)
    return totals[0:1], image_proj_grad, text_proj_grad, totals[1:2], totals[2:3]


def solution(mesh):
    layout = Layout(mesh.shape["dp"], mesh.shape["mp"])
    return jax.shard_map(
        functools.partial(per_device, layout),
        mesh=mesh,
        in_specs=(P(AXES, None), P(AXES, None), P(), P(), P(), P()),
        out_specs=(P(), P(AXES, None), P(AXES, None), P(), P()),
        check_vma=False,
    )
```

```python
import functools
import math

import jax
import jax.numpy as jnp
from jax import lax
from jax.experimental import pallas as pl
from jax.experimental.pallas import tpu as pltpu
from jax.sharding import PartitionSpec as P

F32 = jnp.float32
BF16 = jnp.bfloat16
AXES = ("dp", "mp")


class Layout:
    def __init__(self, dp_size, mp_size):
        self.dp, self.mp = dp_size, mp_size
        self.units = dp_size * mp_size // 2
        self.side = math.isqrt(self.units)
        if self.side * self.side != self.units or self.side % mp_size or self.side & (self.side - 1):
            raise ValueError("unsupported mesh")

    def device(self, unit, core):
        return (2 * (unit // self.mp) + core) * self.mp + unit % self.mp

    def send(self, value, step):
        s = self.side
        pairs = []
        for unit in range(self.units):
            for core in range(2):
                row, column, other = step(*divmod(unit, s), core)
                pairs.append((self.device(unit, core), self.device(row * s + column, other)))
        return lax.ppermute(value, AXES, pairs)

    def along_column(self, value, t):
        return self.send(value, lambda r, c, core: (r ^ t, c, core))

    def along_row(self, value, t):
        return self.send(value, lambda r, c, core: (r, c ^ t, core))

    def exchange(self, value, row_bits, column_bits):
        return self.send(value, lambda r, c, core: (r ^ row_bits, c ^ column_bits, core))

    def sibling(self, value):
        return self.send(value, lambda r, c, core: (r, c, 1 - core))


def tree_sum(values):
    values = list(values)
    while len(values) > 1:
        values = [a + b for a, b in zip(values[::2], values[1::2])]
    return values[0]


def this_core():
    return lax.rem(lax.axis_index("dp"), 2)


def load_projections(image_proj, text_proj, projs, sems):
    core = this_core()
    own = pltpu.make_async_copy(image_proj, projs.at[core], sems.at[0])
    other = pltpu.make_async_copy(text_proj, projs.at[1 - core], sems.at[1])
    own.start()
    other.start()
    return [own, other]


def load_chunk(shards, feats, sems):
    core = this_core()
    rows = shards[0].shape[0]
    copies = []
    for i, shard in enumerate(shards):
        place = pl.ds((core if i < 2 else 1 - core) * rows, rows)
        side = core if i % 2 == 0 else 1 - core
        copies.append(pltpu.make_async_copy(shard, feats.at[side, place], sems.at[i]))
        copies[-1].start()
    return copies


def project(rows, projection):
    raw = jnp.dot(rows, projection, preferred_element_type=F32)
    inverse = lax.rsqrt(jnp.sum(raw * raw, axis=-1, keepdims=True) + 1e-06)
    return raw * inverse, inverse


def project_kernel(image_proj, text_proj, *refs):
    shards, (own_chunk, own_unit, own_inverse, other_half, feats, projs, sems) = refs[:4], refs[4:]
    copies = load_chunk(shards, feats, sems.at[pl.ds(2, 4)])
    copies += load_projections(image_proj, text_proj, projs, sems.at[pl.ds(0, 2)])
    for copy in copies:
        copy.wait()
    unit, _ = project(feats[1], projs[1])
    other_half[...] = unit.astype(BF16)
    unit, inverse = project(feats[0], projs[0])
    own_unit[...] = unit
    own_inverse[...] = jnp.broadcast_to(inverse, own_inverse.shape)
    own_chunk[...] = feats[0]


def project_chunk(image_proj, text_proj, shards, from_arguments):
    rows, width = shards[0].shape
    rows = 2 * rows
    anywhere = pl.BlockSpec(memory_space=pl.ANY)
    hbm = pl.BlockSpec(memory_space=pltpu.HBM)
    vmem = pl.BlockSpec(memory_space=pltpu.VMEM)
    return pl.pallas_call(
        project_kernel,
        out_shape=[
            jax.ShapeDtypeStruct((rows, width), BF16),
            jax.ShapeDtypeStruct((rows, width), F32),
            jax.ShapeDtypeStruct((rows, 128), F32),
            jax.ShapeDtypeStruct((rows, width), BF16),
        ],
        in_specs=[hbm] * 2 + [hbm if from_arguments else anywhere] * 2 + [anywhere] * 2,
        out_specs=[vmem] * 4,
        scratch_shapes=[
            pltpu.VMEM((2, rows, width), BF16),
            pltpu.VMEM((2, width, width), BF16),
            pltpu.SemaphoreType.DMA((6,)),
        ],
        compiler_params=pltpu.CompilerParams(
            vmem_limit_bytes=4 * width * width + 24 * rows * width + 4 * 1024 * 1024
        ),
        cost_estimate=pl.CostEstimate(
            flops=4 * rows * width * width,
            bytes_accessed=4 * width * width + 12 * rows * width,
            transcendentals=2 * rows,
        ),
        name="project",
    )(image_proj, text_proj, *shards)


def pair_terms(cosine, scale, bias, masked):
    logits = scale * cosine + bias
    raised = jnp.exp(logits)
    total = 1.0 + raised
    inverse = 1.0 / total
    losses = jnp.log(total) + (raised - (total - 1.0)) * inverse
    pair_grads = raised * inverse
    if masked:
        equal = lax.broadcasted_iota(jnp.int32, cosine.shape, 0) == lax.broadcasted_iota(
            jnp.int32, cosine.shape, 1
        )
        losses = jnp.where(equal, jnp.log1p(jnp.exp(-logits)), losses)
        pair_grads = jnp.where(equal, -inverse, pair_grads)
    return losses, pair_grads


def lane_sums(values):
    total = jnp.sum(values, axis=0, keepdims=True)
    return sum(total[:, j : j + 128] for j in range(0, total.shape[1], 128))


def block_kernel(side, mp_size, scalars, image_proj, text_proj, *refs):
    last_shards, refs = refs[:4], refs[4:]
    own_chunks, refs = refs[: side - 1], refs[side - 1 :]
    own_units, refs = refs[: side - 1], refs[side - 1 :]
    own_inverses, refs = refs[: side - 1], refs[side - 1 :]
    other_halves, refs = refs[: side - 1], refs[side - 1 :]
    orders = part_orders(side)
    results, refs = refs[: 2 * len(orders)], refs[2 * len(orders) :]
    stats, projs, last, feats, units, inverses, other_half, dy, grad, pieces, moving, sems = refs
    rows, width = dy.shape
    chunk_rows = rows // side
    rest = rows - chunk_rows
    dp_index, mp_index = lax.axis_index("dp"), lax.axis_index("mp")
    unit_index = dp_index // 2 * mp_size + mp_index
    unit_row, unit_column = unit_index // side, lax.rem(unit_index, side)
    scale, bias = scalars[0], scalars[1]

    count = 6

    def start(source, target):
        nonlocal count
        copy = pltpu.make_async_copy(source, target, sems.at[count])
        copy.start()
        count += 1
        return copy

    def places(i):
        return pl.ds(i * chunk_rows, chunk_rows)

    first_copies = load_chunk(last_shards, last, sems.at[pl.ds(2, 4)])
    first_copies += load_projections(image_proj, text_proj, projs, sems.at[pl.ds(0, 2)])
    other_copies = [start(other_halves[i], other_half.at[places(i)]) for i in range(side - 1)]
    unit_copies = [start(own_units[i], units.at[places(i)]) for i in range(side - 1)]
    unit_copies += [start(own_inverses[i], inverses.at[places(i)]) for i in range(side - 1)]
    feat_copies = [start(own_chunks[i], feats.at[places(i)]) for i in range(side - 1)]

    for copy in first_copies:
        copy.wait()
    unit, _ = project(last[1], projs[1])
    other_half[rest:, :] = unit.astype(BF16)
    unit, inverse = project(last[0], projs[0])
    units[rest:, :] = unit
    inverses[rest:, :] = jnp.broadcast_to(inverse, (chunk_rows, 128))
    feats[rest:, :] = last[0]
    for copy in other_copies + unit_copies:
        copy.wait()

    def cosines(i):
        half = units[i * chunk_rows : (i + 1) * chunk_rows, :].astype(BF16)
        return lax.dot_general(
            half, other_half[...], (((1,), (1,)), ((), ())), preferred_element_type=F32
        )

    total = None
    cosine = cosines(0)
    for i in range(side):
        following = cosines(i + 1) if i + 1 < side else None
        if i == 0:
            terms = [
                pair_terms(cosine[:, :chunk_rows], scale, bias, True),
                pair_terms(cosine[:, chunk_rows:], scale, bias, False),
            ]
            losses, pair_grads = [jnp.concatenate(x, axis=1) for x in zip(*terms)]
        else:
            losses, pair_grads = pair_terms(cosine, scale, bias, False)
        half_grads = pair_grads.astype(BF16)
        sums = [lane_sums(losses), lane_sums(pair_grads * cosine) * scale, lane_sums(pair_grads)]
        sums = jnp.concatenate(sums, axis=1)
        total = sums if total is None else total + sums
        inner = jnp.sum(half_grads.astype(F32) * cosine, axis=-1, keepdims=True)
        grads = jnp.dot(half_grads, other_half[...], preferred_element_type=F32)
        place = slice(i * chunk_rows, (i + 1) * chunk_rows)
        grads = (grads - units[place, :] * inner) * (scale * inverses[place, 0:1])
        dy[place, :] = grads.astype(BF16)
        cosine = following
    stats[0:1, :] = total

    for copy in feat_copies:
        copy.wait()
    step = width // 3
    for j in range(0, width, step):
        grad[j : j + step, :] = lax.dot_general(
            feats[:, j : j + step], dy[...], (((0,), (0,)), ((), ())), preferred_element_type=F32
        )

    sums = stats[0:1, :]
    stats[...] = jnp.broadcast_to(sums, stats.shape)
    chunk = width // side
    out_rows = chunk // (2 * side)
    piece_rows = pieces.shape[0] // side**2
    for unit in range(side**2):
        row, column = divmod(unit, side)
        for core in range(2):
            source = row * chunk + shard_of(column, core, mp_size) * out_rows
            target = unit * piece_rows + core * out_rows
            pieces[target : target + out_rows, :] = grad[source : source + out_rows, :]
        if piece_rows > 2 * out_rows:
            target = unit * piece_rows + 2 * out_rows
            pieces[target : (unit + 1) * piece_rows, :] = jnp.zeros(
                (piece_rows - 2 * out_rows, width), F32
            )
    half = side**2 // 2
    part_width = width // len(orders)
    moving[half * piece_rows :, :] = stat_rows(sums, part_width)
    for g, order in enumerate(orders):
        own, message = results[2 * g : 2 * g + 2]
        columns = slice(g * part_width, (g + 1) * part_width)
        for p in range(2 * half):
            row, column = relative_unit(order, p)
            unit = jnp.bitwise_xor(unit_row, row) * side + jnp.bitwise_xor(unit_column, column)
            block = pieces[pl.ds(pl.multiple_of(unit * piece_rows, 8), piece_rows), columns]
            target = p % half * piece_rows
            (own if p < half else moving)[target : target + piece_rows, :] = block
        message[...] = moving[: message.shape[0], :].astype(BF16)


def part_orders(side):
    bits = [1 << i for i in range(side.bit_length() - 1)]
    rows, columns = [(b, 0) for b in bits], [(0, b) for b in bits]
    return [
        rows + columns[::-1],
        [rows[-1], columns[0]] + rows[:-1] + columns[1:],
        [columns[0]] + rows + columns[1:],
    ]


def relative_unit(order, position):
    row = column = 0
    for i, step in enumerate(reversed(order)):
        if position >> i & 1:
            row, column = row | step[0], column | step[1]
    return row, column


def shard_of(column, core, mp_size):
    return column // mp_size * 2 * mp_size + core * mp_size + column % mp_size


def stat_rows(sums, width):
    part0 = sums.astype(BF16).astype(F32)
    part1 = (sums - part0).astype(BF16).astype(F32)
    part2 = sums - part0 - part1
    line = lax.broadcasted_iota(jnp.int32, (8, sums.shape[1]), 0)
    parts = jnp.where(line == 0, part0, jnp.where(line == 1, part1, jnp.where(line == 2, part2, 0.0)))
    if width > sums.shape[1]:
        parts = jnp.concatenate([parts, jnp.zeros((8, width - sums.shape[1]), F32)], axis=1)
    return parts


def block_grads(layout, scalars, image_proj, text_proj, last_shards, projected):
    side = layout.side
    chunk_rows, width = projected[0][0].shape
    rows = side * chunk_rows
    anywhere = pl.BlockSpec(memory_space=pl.ANY)
    vmem = pl.BlockSpec(memory_space=pltpu.VMEM)
    operands = [image_proj, text_proj, *last_shards]
    operands += [x for column in zip(*projected) for x in column]
    parts = len(part_orders(side))
    part_width = width // parts
    piece_rows = (width // layout.units + 7) // 8 * 8
    half_rows = layout.units // 2 * piece_rows
    out_shape = []
    for g in range(parts):
        out_shape.append(jax.ShapeDtypeStruct((half_rows, part_width), F32))
        out_shape.append(jax.ShapeDtypeStruct((half_rows if g else half_rows + 8, part_width), BF16))
    out_shape.append(jax.ShapeDtypeStruct((8, part_width), F32))
    needed = 6 * width * width + 14 * rows * width + 16 * half_rows * width
    needed += 12 * chunk_rows * rows + 2 * 1024 * 1024
    return pl.pallas_call(
        functools.partial(block_kernel, side, layout.mp),
        out_shape=out_shape,
        in_specs=[pl.BlockSpec(memory_space=pltpu.SMEM)]
        + [pl.BlockSpec(memory_space=pltpu.HBM)] * 2
        + [anywhere] * (len(operands) - 2),
        out_specs=[vmem] * len(out_shape),
        scratch_shapes=[
            pltpu.VMEM((2, width, width), BF16),
            pltpu.VMEM((2, chunk_rows, width), BF16),
            pltpu.VMEM((rows, width), BF16),
            pltpu.VMEM((rows, width), F32),
            pltpu.VMEM((rows, 128), F32),
            pltpu.VMEM((rows, width), BF16),
            pltpu.VMEM((rows, width), BF16),
            pltpu.VMEM((width, width), F32),
            pltpu.VMEM((2 * half_rows, width), F32),
            pltpu.VMEM((half_rows + 8, part_width), F32),
            pltpu.SemaphoreType.DMA((len(operands),)),
        ],
        compiler_params=pltpu.CompilerParams(vmem_limit_bytes=min(needed, 60 * 1024 * 1024)),
        cost_estimate=pl.CostEstimate(
            flops=2 * rows * width * (2 * rows + width) + 4 * chunk_rows * width * width,
            bytes_accessed=12 * rows * width + 4 * width * width,
            transcendentals=3 * rows * rows,
        ),
        name="block",
    )(scalars, *operands)


def halve_kernel(own, arrived, *refs):
    rows, half = own.shape[0], own.shape[0] // 2
    total = arrived[...].astype(F32)
    keep, message = refs[-2], refs[-1]
    moved = own[half:, :] + total[half:rows, :]
    keep[...] = own[:half, :] + total[:half, :]
    if len(refs) > 2:
        own_stats, stats = refs[0], refs[1]
        parts = total[rows:, :]
        sums = own_stats[0:1, :] + (parts[0:1, :] + parts[1:2, :] + parts[2:3, :])
        stats[...] = jnp.broadcast_to(sums, stats.shape)
        moved = jnp.concatenate([moved, stat_rows(sums, own.shape[1])], axis=0)
    message[...] = moved.astype(BF16)


def halve(own, arrived, *own_stats):
    rows, width = own.shape
    half = rows // 2
    vmem = pl.BlockSpec(memory_space=pltpu.VMEM)
    stats = [jax.ShapeDtypeStruct(x.shape, F32) for x in own_stats]
    out_shape = [
        *stats,
        jax.ShapeDtypeStruct((half, width), F32),
        jax.ShapeDtypeStruct((half + 8 * len(stats), width), BF16),
    ]
    return pl.pallas_call(
        halve_kernel,
        out_shape=out_shape,
        in_specs=[vmem] * (2 + len(stats)),
        out_specs=[vmem] * len(out_shape),
        compiler_params=pltpu.CompilerParams(vmem_limit_bytes=12 * 1024 * 1024),
        name="halve",
    )(own, arrived, *own_stats)


def per_device(layout, image_feats, text_feats, image_proj, text_proj, log_scale, logit_bias):
    side = layout.side
    own_rows, width = image_feats.shape
    devices = layout.dp * layout.mp
    out_rows = width // devices
    batch_total = own_rows * devices
    is_image = lax.axis_index("dp") % 2 == 0

    scalars = jnp.concatenate([jnp.exp(log_scale), logit_bias])

    images, texts, swapped, projected = {0: image_feats}, {0: text_feats}, {}, {}

    def swap(t):
        swapped[t] = layout.sibling(images[t]), layout.sibling(texts[t])

    def project_next(t):
        shards = [images[t], texts[t], *swapped[t]]
        projected[t] = project_chunk(image_proj, text_proj, shards, t == 0)

    last = side - 1
    bit = side // 2
    while bit > 1:
        for t in list(images):
            images[t ^ bit] = layout.along_row(images[t], bit)
            texts[t ^ bit] = layout.along_column(texts[t], bit)
        bit //= 2
    sources = [t for t in images if t]
    images[1] = layout.along_row(image_feats, 1)
    texts[1] = layout.along_column(text_feats, 1)
    swap(0)
    project_next(0)
    images, texts, projected = lax.optimization_barrier((images, texts, projected))
    for t in sources:
        images[t ^ 1] = layout.along_row(images[t], 1)
        texts[t ^ 1] = layout.along_column(texts[t], 1)
    for t in range(1, last):
        swap(t)
        project_next(t)
    images[last], texts[last], projected = lax.optimization_barrier(
        (images[last], texts[last], projected)
    )
    swap(last)
    results = block_grads(
        layout,
        scalars,
        image_proj,
        text_proj,
        [images[last], texts[last], *swapped[last]],
        [projected[t] for t in range(last)],
    )
    orders = part_orders(side)
    owns, messages = list(results[0:-1:2]), list(results[1:-1:2])
    stats = [results[-1]]

    steps = len(orders[0])
    for step in range(steps):
        arrived = [
            layout.exchange(message, *order[step]) for message, order in zip(messages, orders)
        ]
        if step + 1 < steps:
            for g in range(len(orders)):
                *some, owns[g], messages[g] = halve(owns[g], arrived[g], *([] if g else stats))
                stats = some if g == 0 else stats
    last_rows = 2 * out_rows
    total = jnp.concatenate(
        [own[:last_rows] + x[:last_rows].astype(F32) for own, x in zip(owns, arrived)], axis=1
    )
    parts = arrived[0][owns[0].shape[0] :].astype(F32)
    stat_total = stats[0][0] + (parts[0] + parts[1] + parts[2])

    upper, lower = total[:out_rows], total[out_rows:]
    keep, give = jnp.where(is_image, upper, lower), jnp.where(is_image, lower, upper)
    got = layout.sibling(give)
    image_proj_grad = jnp.where(is_image, keep, got)
    text_proj_grad = jnp.where(is_image, got, keep)
    stat_total = stat_total + layout.sibling(stat_total)
    totals = jnp.sum(stat_total.reshape(3, 128), axis=1) * (0.5 / batch_total)
    return totals[0:1], image_proj_grad, text_proj_grad, totals[1:2], totals[2:3]


def solution(mesh):
    layout = Layout(mesh.shape["dp"], mesh.shape["mp"])
    return jax.shard_map(
        functools.partial(per_device, layout),
        mesh=mesh,
        in_specs=(P(AXES, None), P(AXES, None), P(), P(), P(), P()),
        out_specs=(P(), P(AXES, None), P(AXES, None), P(), P()),
        check_vma=False,
    )
```
